128 devices in a mesh: front: 32 (over z, y, x_hi), row: 2 (over core), col: 2 (over x_lo).
Axes of the slice: x: 4 (x_hi: 2, x_lo: 2; x = x_hi * 2 + x_lo), y: 4, z: 4, core: 2. Of those that a mesh axis runs over, the one named last changes fastest.
Arguments:
- bounds: int32 [32], P('front'), may hold values from 3072 to 5120, as said below
- block_map: int32 [32, 40], P('front', 'row'), may hold values from 0 to 1535, as said below
- pivot_inverse: bfloat16 [32, 1024, 1024], P('front', 'col', 'row'), may hold values from -0.1875 to 0.1875
- upper_block: bfloat16 [32, 1024, 5120], P('front', 'row', 'col'), may hold values from -0.078125 to 0.078125
- lower_block: bfloat16 [32, 5120, 1024], P('front', 'row', 'col'), may hold values from -0.1875 to 0.1875
- trailing_block: bfloat16 [32, 5120, 5120], P('front', 'row', 'col'), may hold values from -0.078125 to 0.078125
- sketch: bfloat16 [5120, 512], P('col'), may hold values from -6 to 6
- basis: bfloat16 [32, 6144, 512], P('front', 'row'), may hold values from -0.078125 to 0.078125
Outputs:
- coefficients: float32 [32, 512, 512], P('front', None, 'col')
- residual: float32 [32, 6144, 512], P('front', 'row', 'col')
The draws below stay inside these ranges and needn't reach their ends.
Inputs may be any that keep to these rules, and one draw needn't show every extreme that they name: `bounds`: each is a multiple of 128; some front has exactly 5120. `block_map`: entries for blocks at or beyond a front's boundary are ignored. Within one front all entries are distinct. Owner (g, r) holds parent blocks g * 48 + r * 24 to g * 48 + (r + 1) * 24 - 1; an entry held by the device at index r of row names a block of an owner with the same r. Among the 20 entries held by one device, at most 1 name blocks of one owner, and some device has exactly 1 for some owner.
All inputs are finite; a program needn't handle non-finite values.
Results may differ from the reference program's by a relative error of at most 0.0042.
Values may be sent and summed in bfloat16 or wider, within the bound.
A program may use at most 128 MiB of HBM per device.

```python
import jax
import jax.numpy as jnp
from jax import lax

PIVOT = 1024
BMAX = 5120
BMIN = 3072
BLOCK = 128
SKETCH = 512
RANK = 512
FRONT_DEV = 1
PBLK_DEV = 24
FRONTS = 32
BLK = 40
BLK_DEV = 20
DESTS = 32
CAP = 1
PARENTS = 32
PROWS = 6144


def draw_bounds(key, part):
    block_count = BMAX // BLOCK
    lowest = BMIN // BLOCK
    drawn_blocks = jax.random.randint(jax.random.fold_in(key, 11), (FRONTS,), lowest, block_count + 1)
    widest = jax.random.randint(jax.random.fold_in(key, 12), (), 0, FRONTS)
    chosen = jnp.where(jnp.arange(FRONTS) == widest, block_count, drawn_blocks)
    return (chosen * BLOCK).astype(jnp.int32)


def draw_block_map(key, part):
    order_key = jax.random.fold_in(key, 21)
    row_total = BLK // BLK_DEV
    sender_total = DESTS * row_total

    def shuffle_one(sender_id):
        return jax.random.permutation(jax.random.fold_in(order_key, sender_id), DESTS)
    orders = jax.vmap(shuffle_one)(jnp.arange(sender_total, dtype=jnp.int32)).astype(jnp.int32)
    offsets = jax.random.randint(jax.random.fold_in(key, 22), (FRONTS, DESTS), 0, PBLK_DEV).astype(jnp.int32)
    fronts = jnp.arange(FRONTS, dtype=jnp.int32)[:, None]
    columns = jnp.arange(BLK, dtype=jnp.int32)[None, :]
    row_of = columns // BLK_DEV
    sender = fronts // FRONT_DEV * row_total + row_of
    order_pos = fronts % FRONT_DEV * BLK_DEV + columns % BLK_DEV
    target = orders[sender, order_pos // CAP]
    local_block = (offsets[fronts, target] + order_pos % CAP) % PBLK_DEV
    return (target * (PBLK_DEV * row_total) + row_of * PBLK_DEV + local_block).astype(jnp.int32)


def steps_of(own_key, shape, shards, low, top_value):
    factor_of = 1.0
    for position, shards_of in shards:
        steps = jax.random.uniform(jax.random.fold_in(jax.random.fold_in(own_key, 6), position), (shards_of,), jnp.float32, low / len(shards), top_value / len(shards))
        factor_of = factor_of * jnp.repeat(jnp.exp(steps), shape[position] // shards_of).reshape((-1,) + (1,) * (len(shape) - 1 - position))
    return factor_of


def noise(key, extent, deviation, reach, cuts=(), held_as=jnp.bfloat16):
    entries = deviation * jax.random.normal(key, extent, jnp.float32)
    if cuts:
        entries = entries * steps_of(key, extent, cuts, -0.22, 0.18)
    return jnp.clip(entries, -reach, reach).astype(held_as)


def setup_inputs(seed: int = 0) -> dict:
    streams_of = jax.random.split(jax.random.key(seed), 9)
    return {
        "bounds": draw_bounds(jax.random.fold_in(streams_of[8], 71), 0),
        "block_map": draw_block_map(jax.random.fold_in(streams_of[8], 71), 0),
        "pivot_inverse": noise(streams_of[2], (FRONTS, PIVOT, PIVOT), PIVOT ** -0.5, 0.1875, ((0, 32), (1, 2), (2, 2))),
        "upper_block": noise(streams_of[3], (FRONTS, PIVOT, BMAX), BMAX ** -0.5, 0.078125, ((0, 32), (1, 2), (2, 2))),
        "lower_block": noise(streams_of[4], (FRONTS, BMAX, PIVOT), PIVOT ** -0.5, 0.1875, ((0, 32), (1, 2), (2, 2))),
        "trailing_block": noise(streams_of[5], (FRONTS, BMAX, BMAX), BMAX ** -0.5, 0.078125, ((0, 32), (1, 2), (2, 2))),
        "sketch": noise(streams_of[6], (BMAX, SKETCH), 1.0, 6.0, ((0, 2),)),
        "basis": noise(streams_of[7], (PARENTS, PROWS, RANK), PROWS ** -0.5, 0.078125, ((0, 32), (1, 2))),
    }


def reference(bounds, block_map, pivot_inverse, upper_block, lower_block, trailing_block, sketch, basis):
    positions = jnp.arange(BMAX, dtype=jnp.int32)

    def one_front(pieces):
        boundary, inverse, upper_part, lower_part, trailing = pieces
        masked = sketch * (positions < boundary).astype(jnp.bfloat16)[:, None]
        pivot_rows = jnp.dot(upper_part, masked, preferred_element_type=jnp.float32).astype(jnp.bfloat16)
        solved = jnp.dot(inverse, pivot_rows, preferred_element_type=jnp.float32).astype(jnp.bfloat16)
        return jnp.dot(trailing, masked, preferred_element_type=jnp.float32) - jnp.dot(lower_part, solved, preferred_element_type=jnp.float32)

    sketched = lax.map(one_front, (bounds, pivot_inverse, upper_block, lower_block, trailing_block))
    total_blocks = PARENTS * PROWS // BLOCK
    blocks = sketched.reshape(FRONTS * BLK, BLOCK, SKETCH)
    starts = jnp.arange(BLK, dtype=jnp.int32) * BLOCK
    live_rows = (starts[None, :] < bounds[:, None]).reshape(-1)
    targets = jnp.where(live_rows, block_map.reshape(-1), total_blocks).astype(jnp.int32)
    parent = jnp.zeros((total_blocks, BLOCK, SKETCH), jnp.float32).at[targets].add(blocks, mode="drop")
    parent = parent.reshape(PARENTS, PROWS, SKETCH)
    rounded = lax.optimization_barrier(parent.astype(jnp.bfloat16)).astype(jnp.float32)
    basis_wide = basis.astype(jnp.float32)
    coefficients = jnp.einsum("prq,prk->pqk", basis_wide, rounded, precision=lax.Precision.HIGHEST)
    coeff_rounded = lax.optimization_barrier(coefficients.astype(jnp.bfloat16)).astype(jnp.float32)
    projected = jnp.einsum("prq,pqk->prk", basis_wide, coeff_rounded, precision=lax.Precision.HIGHEST)
    return coefficients, parent - projected
```

```python
import jax
import jax.numpy as jnp
from jax import lax
from jax.experimental import pallas as pl
from jax.experimental.pallas import tpu as pltpu
from jax.sharding import PartitionSpec as P

BLOCK = 128
MESH = pl.DeviceIdType.MESH
F32 = jnp.float32
BF16 = jnp.bfloat16
STEP, UNSTEP, FRONTS = 13, 5, 32


def parts(front):
    return front // 8, (front // 2) % 4, front % 2


def moved(front, offset, sign):
    (z, y, x), (dz, dy, dx) = parts(front), parts(offset)
    return ((z + sign * dz + 4) % 4) * 8 + ((y + sign * dy + 4) % 4) * 2 + (x + dx) % 2


def slot_of(dest, source):
    (z, y, x), (sz, sy, sx) = parts(dest), parts(source)
    offset = ((z - sz + 4) % 4) * 8 + ((y - sy + 4) % 4) * 2 + (x + sx) % 2
    return (offset * UNSTEP) % FRONTS


def sketch_kernel(
    tab,
    sk_hbm, up_hbm, pi_hbm, lo_hbm, tr_hbm,
    land,
    sk, up, pi, lo, tr, total, uown, usend, urecv, piv, vown, vrecv, solved, keep, pay, precv, summed, sbuf,
    ld, us, ur, vs, vr, ps, pr, ss, sr,
):
    me, row, col = lax.axis_index("front"), lax.axis_index("row"), lax.axis_index("col")
    blocks = total.shape[0]
    mate = {"col": 1 - col}
    twin = {"row": 1 - row}

    def peer(slot):
        offset = (slot * STEP) % FRONTS
        return {"front": moved(me, offset, 1), "col": (col + offset % 2) % 2}

    loads = [
        pltpu.make_async_copy(sk_hbm, sk, ld.at[0]),
        pltpu.make_async_copy(up_hbm, up, ld.at[1]),
        pltpu.make_async_copy(pi_hbm, pi, ld.at[2]),
    ]
    tiles = tr.shape[0]
    for t in range(tiles):
        loads.append(pltpu.make_async_copy(tr_hbm.at[t], tr.at[t], ld.at[3 + t]))
    loads.append(pltpu.make_async_copy(lo_hbm, lo, ld.at[3 + tiles]))
    for copy in loads:
        copy.start()

    barrier = pltpu.get_barrier_semaphore()
    pl.semaphore_signal(barrier, inc=1, device_id=mate, device_id_type=MESH)
    pl.semaphore_signal(barrier, inc=1, device_id=twin, device_id_type=MESH)

    @pl.loop(1, FRONTS)
    def _(slot):
        pl.semaphore_signal(barrier, inc=1, device_id=peer(slot), device_id_type=MESH)

    loads[0].wait()
    height = sk.shape[0]
    bound = tab[0]
    step = 512

    @pl.loop(0, height // step)
    def _(i):
        at = pl.ds(pl.multiple_of(i * step, step), step)
        places = lax.broadcasted_iota(jnp.int32, (step, sk.shape[1]), 0) + (col * height + i * step)
        sk[at, :] = jnp.where(places < bound, sk[at, :].astype(F32), 0.0).astype(BF16)

    half = sk.shape[1] // 2
    loads[1].wait()
    usends = []
    for j in range(2):
        uown[j] = jnp.dot(up[...], sk[:, j * half : (j + 1) * half], preferred_element_type=F32)
        usend[j] = uown[j].astype(BF16)
        if j == 0:
            pl.semaphore_wait(barrier, FRONTS + 1)
        copy = pltpu.make_async_remote_copy(
            src_ref=usend.at[j], dst_ref=urecv.at[j], send_sem=us.at[j], recv_sem=ur.at[j],
            device_id=mate, device_id_type=MESH,
        )
        copy.start()
        usends.append(copy)

    per = blocks // tiles
    for t in range(tiles):
        loads[3 + t].wait()

        part = jnp.dot(tr[t], sk[...], preferred_element_type=F32)
        total[t * per : (t + 1) * per] = part.reshape(per, BLOCK, 2 * half)

    loads[2].wait()
    loads[3 + tiles].wait()
    vsends = []
    for j in range(2):
        usends[j].wait_recv()
        piv[...] = (uown[j] + urecv[j].astype(F32)).astype(BF16)
        vown[j] = jnp.dot(pi[...], piv[...], preferred_element_type=F32)
        copy = pltpu.make_async_remote_copy(
            src_ref=vown.at[j], dst_ref=vrecv.at[j], send_sem=vs.at[j], recv_sem=vr.at[j],
            device_id=twin, device_id_type=MESH,
        )
        copy.start()
        vsends.append(copy)
    for j in range(2):
        vsends[j].wait_recv()
        solved[:, j * half : (j + 1) * half] = (vown[j] + vrecv[j]).astype(BF16)

    def to_mate(p):
        return pltpu.make_async_remote_copy(
            src_ref=pay.at[p], dst_ref=precv.at[p], send_sem=ps.at[p], recv_sem=pr.at[p],
            device_id=mate, device_id_type=MESH,
        )

    def to_owner(slot):
        return pltpu.make_async_remote_copy(
            src_ref=sbuf.at[slot], dst_ref=land.at[slot], send_sem=ss.at[slot], recv_sem=sr.at[slot],
            device_id=peer(slot), device_id_type=MESH,
        )

    @pl.loop(0, blocks)
    def _(p):
        block = tab[1 + p]
        front = total[block] - jnp.dot(lo[block], solved[...], preferred_element_type=F32)
        left, right = front[:, :half], front[:, half:]
        stays = jnp.broadcast_to((tab[1 + blocks + p] + col) % 2, left.shape) == 0
        keep[p] = jnp.where(stays, left, right)
        pay[p] = jnp.where(stays, right, left).astype(BF16)
        to_mate(p).start()

    def fill(slot):
        sbuf[slot] = summed[tab[1 + 2 * blocks + slot]]

    def add(p):
        to_mate(p).wait_recv()
        summed[p] = (keep[p] + precv[p].astype(F32)).astype(BF16)
        fill(p)

    add(0)
    own = pltpu.make_async_copy(sbuf.at[0], land.at[0], ss.at[0])
    own.start()

    @pl.loop(1, blocks)
    def _(p):
        add(p)
        to_owner(p).start()

    @pl.loop(blocks, FRONTS)
    def _(slot):
        fill(slot)
        to_owner(slot).start()

    for j in range(2):
        usends[j].wait_send()
        vsends[j].wait_send()

    @pl.loop(0, blocks)
    def _(p):
        to_mate(p).wait_send()

    own.wait()

    @pl.loop(1, FRONTS)
    def _(slot):
        to_owner(slot).wait()


def sketch_call(tab, sketch, upper, pinv, lower, trailing):
    height, width = sketch.shape
    blocks = lower.shape[0] // BLOCK
    pivot = pinv.shape[0]
    half = width // 2
    tiles = 5
    hbm = pl.BlockSpec(memory_space=pl.ANY)
    return pl.pallas_call(
        sketch_kernel,
        out_shape=jax.ShapeDtypeStruct((FRONTS, BLOCK, half), BF16),
        in_specs=[pl.BlockSpec(memory_space=pltpu.SMEM)] + [hbm] * 5,
        out_specs=hbm,
        scratch_shapes=[
            pltpu.VMEM((height, width), BF16),
            pltpu.VMEM(upper.shape, BF16),
            pltpu.VMEM(pinv.shape, BF16),
            pltpu.VMEM((blocks, BLOCK, pivot), BF16),
            pltpu.VMEM((tiles, trailing.shape[0] // tiles, height), BF16),
            pltpu.VMEM((blocks, BLOCK, width), F32),
            pltpu.VMEM((2, pivot, half), F32),
            pltpu.VMEM((2, pivot, half), BF16),
            pltpu.VMEM((2, pivot, half), BF16),
            pltpu.VMEM((pivot, half), BF16),
            pltpu.VMEM((2, pivot, half), F32),
            pltpu.VMEM((2, pivot, half), F32),
            pltpu.VMEM((pivot, width), BF16),
            pltpu.VMEM((blocks, BLOCK, half), F32),
            pltpu.VMEM((blocks, BLOCK, half), BF16),
            pltpu.VMEM((blocks, BLOCK, half), BF16),
            pltpu.VMEM((blocks, BLOCK, half), BF16),
            pltpu.VMEM((FRONTS, BLOCK, half), BF16),
            pltpu.SemaphoreType.DMA((4 + tiles,)),
            pltpu.SemaphoreType.DMA((2,)),
            pltpu.SemaphoreType.DMA((2,)),
            pltpu.SemaphoreType.DMA((2,)),
            pltpu.SemaphoreType.DMA((2,)),
            pltpu.SemaphoreType.DMA((blocks,)),
            pltpu.SemaphoreType.DMA((blocks,)),
            pltpu.SemaphoreType.DMA((FRONTS,)),
            pltpu.SemaphoreType.DMA((FRONTS,)),
        ],
        compiler_params=pltpu.CompilerParams(
            collective_id=0, has_side_effects=True, vmem_limit_bytes=52 * 2**20
        ),
        cost_estimate=pl.CostEstimate(flops=10_000_000_000, bytes_accessed=100_000_000, transcendentals=0),
        name="sketch",
    )(
        tab, sketch, upper, pinv,
        lower.reshape(blocks, BLOCK, pivot),
        trailing.reshape(tiles, trailing.shape[0] // tiles, height),
    )


def parent_kernel(tags, land, basis, parent, coeff):
    parent[...] = jnp.zeros_like(parent)
    per = parent.shape[0]

    @pl.loop(0, FRONTS)
    def _(slot):
        tag = tags[slot]

        @pl.when(tag < per)
        def _():
            parent[tag] += land[slot].astype(F32)

    rounded = parent[...].astype(BF16).reshape(per * BLOCK, parent.shape[2])
    coeff[...] = lax.dot_general(
        basis[...], rounded, (((0,), (0,)), ((), ())), preferred_element_type=F32
    )


def parent_call(tags, land, basis):
    rows, rank = basis.shape
    half = land.shape[2]
    vmem = pl.BlockSpec(memory_space=pltpu.VMEM)
    return pl.pallas_call(
        parent_kernel,
        out_shape=(
            jax.ShapeDtypeStruct((rows // BLOCK, BLOCK, half), F32),
            jax.ShapeDtypeStruct((rank, half), F32),
        ),
        in_specs=[pl.BlockSpec(memory_space=pltpu.SMEM), vmem, vmem],
        out_specs=(vmem, vmem),
        compiler_params=pltpu.CompilerParams(vmem_limit_bytes=40 * 2**20),
        name="parent",
    )(tags, land, basis)


def residual_kernel(parent, basis, coeff, out):
    out[...] = parent[...] - jnp.dot(basis[...], coeff[...], preferred_element_type=F32)


def residual_call(parent, basis, coeff):
    rows, rank = basis.shape
    half = parent.shape[1]
    tile = 512
    return pl.pallas_call(
        residual_kernel,
        out_shape=jax.ShapeDtypeStruct((rows, half), F32),
        grid=(rows // tile,),
        in_specs=[
            pl.BlockSpec((tile, half), lambda i: (i, 0)),
            pl.BlockSpec((tile, rank), lambda i: (i, 0)),
            pl.BlockSpec((rank, half), lambda i: (0, 0)),
        ],
        out_specs=pl.BlockSpec((tile, half), lambda i: (i, 0)),
        compiler_params=pltpu.CompilerParams(vmem_limit_bytes=40 * 2**20),
        name="residual",
    )(parent, basis, coeff)


def body(bounds, block_map, pivot_inverse, upper_block, lower_block, trailing_block, sketch, basis):
    me, row = lax.axis_index("front"), lax.axis_index("row")
    blocks = block_map.shape[1]
    per = basis.shape[1] // BLOCK
    per_front = per * lax.axis_size("row")
    boundary = bounds[0]
    entries = block_map.reshape(-1)
    order = jnp.arange(blocks, dtype=jnp.int32)
    slots = jnp.arange(FRONTS, dtype=jnp.int32)
    live = (row * blocks + order) * BLOCK < boundary
    everyone = lax.all_gather(jnp.where(live, entries, -1), "front")

    dest = entries // per_front
    slot = jnp.where(live, slot_of(dest, me), FRONTS + order)
    place = jnp.sum((slot[None, :] < slot[:, None]).astype(jnp.int32), axis=1)
    at = (place[None, :] == order[:, None]).astype(jnp.int32)
    block_at = jnp.sum(at * order[None, :], axis=1)
    turned = jnp.sum(at * ((dest + me) % 2)[None, :], axis=1)
    place_of = jnp.sum(jnp.where(slot[None, :] == slots[:, None], place[None, :], 0), axis=1)
    tab = jnp.concatenate([bounds, block_at, turned, place_of])

    land = sketch_call(
        tab, sketch, upper_block[0], pivot_inverse[0], lower_block[0], trailing_block[0]
    )

    mine = (everyone >= 0) & (everyone // per_front == me)
    tag = jnp.sum(jnp.where(mine, everyone % per - per, 0), axis=1) + per
    source = slot_of(me, slots)
    tags = jnp.sum(jnp.where(source[None, :] == slots[:, None], tag[None, :], 0), axis=1)
    parent, part = parent_call(tags, land, basis[0])
    other = lax.ppermute(part, "row", [(0, 1), (1, 0)])
    coefficients = part + other
    residual = residual_call(
        parent.reshape(per * BLOCK, -1), basis[0], coefficients.astype(BF16)
    )
    return coefficients[None], residual[None]


def solution(mesh):
    placed = (
        P("front"),
        P("front", "row"),
        P("front", "col", "row"),
        P("front", "row", "col"),
        P("front", "row", "col"),
        P("front", "row", "col"),
        P("col", None),
        P("front", "row", None),
    )
    return jax.shard_map(
        body,
        mesh=mesh,
        in_specs=placed,
        out_specs=(P("front", None, "col"), P("front", "row", "col")),
        check_vma=False,
    )
```

```python
import jax
import jax.numpy as jnp
from jax import lax
from jax.experimental import pallas as pl
from jax.experimental.pallas import tpu as pltpu
from jax.sharding import PartitionSpec as P

BLOCK = 128
MESH = pl.DeviceIdType.MESH
F32 = jnp.float32
BF16 = jnp.bfloat16
STEP, UNSTEP, FRONTS = 13, 5, 32


def parts(front):
    return front // 8, (front // 2) % 4, front % 2


def moved(front, offset, sign):
    (z, y, x), (dz, dy, dx) = parts(front), parts(offset)
    return ((z + sign * dz + 4) % 4) * 8 + ((y + sign * dy + 4) % 4) * 2 + (x + dx) % 2


def slot_of(dest, source):
    (z, y, x), (sz, sy, sx) = parts(dest), parts(source)
    offset = ((z - sz + 4) % 4) * 8 + ((y - sy + 4) % 4) * 2 + (x + sx) % 2
    return (offset * UNSTEP) % FRONTS


def sketch_kernel(
    tab, tile,
    sk_hbm, up_hbm, pi_hbm, lo_hbm, tr_hbm,
    land, marks,
    sk, up, pi, lo, tr, total, uown, usend, urecv, piv, vown, vrecv, solved, keep, pay, precv, summed, sbuf,
    ld, us, ur, vs, vr, ps, pr, ss, sr, ms, mr,
):
    me, row, col = lax.axis_index("front"), lax.axis_index("row"), lax.axis_index("col")
    blocks = total.shape[0]
    mate = {"col": 1 - col}
    twin = {"row": 1 - row}

    def peer(slot):
        offset = (slot * STEP) % FRONTS
        return {"front": moved(me, offset, 1), "col": (col + offset % 2) % 2}

    loads = [
        pltpu.make_async_copy(sk_hbm, sk, ld.at[0]),
        pltpu.make_async_copy(up_hbm, up, ld.at[1]),
        pltpu.make_async_copy(pi_hbm, pi, ld.at[2]),
    ]
    tiles = tr.shape[0]
    for t in range(tiles):
        loads.append(pltpu.make_async_copy(tr_hbm.at[t], tr.at[t], ld.at[3 + t]))
    loads.append(pltpu.make_async_copy(lo_hbm, lo, ld.at[3 + tiles]))
    for copy in loads:
        copy.start()

    barrier = pltpu.get_barrier_semaphore()
    pl.semaphore_signal(barrier, inc=1, device_id=mate, device_id_type=MESH)
    pl.semaphore_signal(barrier, inc=1, device_id=twin, device_id_type=MESH)

    @pl.loop(1, FRONTS)
    def _(slot):
        pl.semaphore_signal(barrier, inc=1, device_id=peer(slot), device_id_type=MESH)

    loads[0].wait()
    height = sk.shape[0]
    bound = tab[0]
    step = 512

    @pl.loop(0, height // step)
    def _(i):
        at = pl.ds(pl.multiple_of(i * step, step), step)
        places = lax.broadcasted_iota(jnp.int32, (step, sk.shape[1]), 0) + (col * height + i * step)
        sk[at, :] = jnp.where(places < bound, sk[at, :].astype(F32), 0.0).astype(BF16)

    half = sk.shape[1] // 2
    loads[1].wait()
    usends = []
    for j in range(2):
        uown[j] = jnp.dot(up[...], sk[:, j * half : (j + 1) * half], preferred_element_type=F32)
        usend[j] = uown[j].astype(BF16)
        if j == 0:
            pl.semaphore_wait(barrier, FRONTS + 1)
        copy = pltpu.make_async_remote_copy(
            src_ref=usend.at[j], dst_ref=urecv.at[j], send_sem=us.at[j], recv_sem=ur.at[j],
            device_id=mate, device_id_type=MESH,
        )
        copy.start()
        usends.append(copy)

    def mark(slot):
        return pltpu.make_async_remote_copy(
            src_ref=tile, dst_ref=marks.at[slot], send_sem=ms.at[slot], recv_sem=mr.at[slot],
            device_id=peer(slot), device_id_type=MESH,
        )

    own_mark = pltpu.make_async_copy(tile, marks.at[0], ms.at[0])
    own_mark.start()

    @pl.loop(1, FRONTS)
    def _(slot):
        mark(slot).start()

    per = blocks // tiles
    for t in range(tiles):
        loads[3 + t].wait()
        part = jnp.dot(tr[t], sk[...], preferred_element_type=F32)
        total[t * per : (t + 1) * per] = part.reshape(per, BLOCK, 2 * half)

    loads[2].wait()
    loads[3 + tiles].wait()
    vsends = []
    for j in range(2):
        usends[j].wait_recv()
        piv[...] = (uown[j] + urecv[j].astype(F32)).astype(BF16)
        vown[j] = jnp.dot(pi[...], piv[...], preferred_element_type=F32)
        copy = pltpu.make_async_remote_copy(
            src_ref=vown.at[j], dst_ref=vrecv.at[j], send_sem=vs.at[j], recv_sem=vr.at[j],
            device_id=twin, device_id_type=MESH,
        )
        copy.start()
        vsends.append(copy)
    for j in range(2):
        vsends[j].wait_recv()
        solved[:, j * half : (j + 1) * half] = (vown[j] + vrecv[j]).astype(BF16)

    def to_mate(p):
        return pltpu.make_async_remote_copy(
            src_ref=pay.at[p], dst_ref=precv.at[p], send_sem=ps.at[p], recv_sem=pr.at[p],
            device_id=mate, device_id_type=MESH,
        )

    def to_owner(slot):
        return pltpu.make_async_remote_copy(
            src_ref=sbuf.at[slot], dst_ref=land.at[slot], send_sem=ss.at[slot], recv_sem=sr.at[slot],
            device_id=peer(slot), device_id_type=MESH,
        )

    @pl.loop(0, blocks)
    def _(p):
        block = tab[1 + p]
        front = total[block] - jnp.dot(lo[block], solved[...], preferred_element_type=F32)
        left, right = front[:, :half], front[:, half:]
        stays = jnp.broadcast_to((tab[1 + blocks + p] + col) % 2, left.shape) == 0
        keep[p] = jnp.where(stays, left, right)
        pay[p] = jnp.where(stays, right, left).astype(BF16)
        to_mate(p).start()

    def fill(slot):
        sbuf[slot] = summed[tab[1 + 2 * blocks + slot]]

    def add(p):
        to_mate(p).wait_recv()
        summed[p] = (keep[p] + precv[p].astype(F32)).astype(BF16)
        fill(p)

    add(0)
    own = pltpu.make_async_copy(sbuf.at[0], land.at[0], ss.at[0])
    own.start()

    @pl.loop(1, blocks)
    def _(p):
        add(p)
        to_owner(p).start()

    @pl.loop(blocks, FRONTS)
    def _(slot):
        fill(slot)
        to_owner(slot).start()

    for j in range(2):
        usends[j].wait_send()
        vsends[j].wait_send()

    @pl.loop(0, blocks)
    def _(p):
        to_mate(p).wait_send()

    own.wait()
    own_mark.wait()

    @pl.loop(1, FRONTS)
    def _(slot):
        to_owner(slot).wait()
        mark(slot).wait()


def sketch_call(tab, tile, sketch, upper, pinv, lower, trailing):
    height, width = sketch.shape
    blocks = lower.shape[0] // BLOCK
    pivot = pinv.shape[0]
    half = width // 2
    tiles = 5
    hbm = pl.BlockSpec(memory_space=pltpu.HBM)
    vmem = pl.BlockSpec(memory_space=pltpu.VMEM)
    return pl.pallas_call(
        sketch_kernel,
        out_shape=(
            jax.ShapeDtypeStruct((FRONTS, BLOCK, half), BF16),
            jax.ShapeDtypeStruct((FRONTS,) + tile.shape, jnp.int32),
        ),
        in_specs=[pl.BlockSpec(memory_space=pltpu.SMEM), vmem] + [hbm] * 5,
        out_specs=(vmem, vmem),
        scratch_shapes=[
            pltpu.VMEM((height, width), BF16),
            pltpu.VMEM(upper.shape, BF16),
            pltpu.VMEM(pinv.shape, BF16),
            pltpu.VMEM((blocks, BLOCK, pivot), BF16),
            pltpu.VMEM((tiles, trailing.shape[0] // tiles, height), BF16),
            pltpu.VMEM((blocks, BLOCK, width), F32),
            pltpu.VMEM((2, pivot, half), F32),
            pltpu.VMEM((2, pivot, half), BF16),
            pltpu.VMEM((2, pivot, half), BF16),
            pltpu.VMEM((pivot, half), BF16),
            pltpu.VMEM((2, pivot, half), F32),
            pltpu.VMEM((2, pivot, half), F32),
            pltpu.VMEM((pivot, width), BF16),
            pltpu.VMEM((blocks, BLOCK, half), F32),
            pltpu.VMEM((blocks, BLOCK, half), BF16),
            pltpu.VMEM((blocks, BLOCK, half), BF16),
            pltpu.VMEM((blocks, BLOCK, half), BF16),
            pltpu.VMEM((FRONTS, BLOCK, half), BF16),
            pltpu.SemaphoreType.DMA((4 + tiles,)),
            pltpu.SemaphoreType.DMA((2,)),
            pltpu.SemaphoreType.DMA((2,)),
            pltpu.SemaphoreType.DMA((2,)),
            pltpu.SemaphoreType.DMA((2,)),
            pltpu.SemaphoreType.DMA((blocks,)),
            pltpu.SemaphoreType.DMA((blocks,)),
            pltpu.SemaphoreType.DMA((FRONTS,)),
            pltpu.SemaphoreType.DMA((FRONTS,)),
            pltpu.SemaphoreType.DMA((FRONTS,)),
            pltpu.SemaphoreType.DMA((FRONTS,)),
        ],
        compiler_params=pltpu.CompilerParams(
            collective_id=0, has_side_effects=True, vmem_limit_bytes=50 * 2**20
        ),
        cost_estimate=pl.CostEstimate(flops=10_000_000_000, bytes_accessed=100_000_000, transcendentals=0),
        name="sketch",
    )(
        tab, tile, sketch, upper, pinv,
        lower.reshape(blocks, BLOCK, pivot),
        trailing.reshape(tiles, trailing.shape[0] // tiles, height),
    )


def parent_kernel(tags, land, basis, parent, coeff):
    parent[...] = jnp.zeros_like(parent)
    per = parent.shape[0]

    @pl.loop(0, FRONTS)
    def _(slot):
        tag = tags[slot]

        @pl.when(tag < per)
        def _():
            parent[tag] += land[slot].astype(F32)

    rounded = parent[...].astype(BF16).reshape(per * BLOCK, parent.shape[2])
    coeff[...] = lax.dot_general(
        basis[...], rounded, (((0,), (0,)), ((), ())), preferred_element_type=F32
    )


def parent_call(tags, land, basis):
    rows, rank = basis.shape
    half = land.shape[2]
    vmem = pl.BlockSpec(memory_space=pltpu.VMEM)
    return pl.pallas_call(
        parent_kernel,
        out_shape=(
            jax.ShapeDtypeStruct((rows // BLOCK, BLOCK, half), F32),
            jax.ShapeDtypeStruct((rank, half), F32),
        ),
        in_specs=[pl.BlockSpec(memory_space=pltpu.SMEM), vmem, vmem],
        out_specs=(vmem, vmem),
        compiler_params=pltpu.CompilerParams(vmem_limit_bytes=40 * 2**20),
        name="parent",
    )(tags, land, basis)


def residual_kernel(parent, basis, part, other, out, coeff, tile, sems):
    total = part[...] + other[...]
    coeff[...] = total
    rounded = total.astype(BF16)
    rows = tile.shape[1]
    copies = []
    for i in range(parent.shape[0] // rows):
        if i >= 2:
            copies[i - 2].wait()
        at = pl.ds(i * rows, rows)
        tile[i % 2] = parent[at, :] - jnp.dot(basis[at, :], rounded, preferred_element_type=F32)
        copy = pltpu.make_async_copy(tile.at[i % 2], out.at[at, :], sems.at[i % 2])
        copy.start()
        copies.append(copy)
    copies[-2].wait()
    copies[-1].wait()


def residual_call(parent, basis, part, other):
    rows, rank = basis.shape
    half = parent.shape[1]
    vmem = pl.BlockSpec(memory_space=pltpu.VMEM)
    return pl.pallas_call(
        residual_kernel,
        out_shape=(
            jax.ShapeDtypeStruct((rows, half), F32),
            jax.ShapeDtypeStruct((rank, half), F32),
        ),
        in_specs=[vmem] * 4,
        out_specs=(pl.BlockSpec(memory_space=pltpu.HBM), vmem),
        scratch_shapes=[pltpu.VMEM((2, 512, half), F32), pltpu.SemaphoreType.DMA((2,))],
        compiler_params=pltpu.CompilerParams(vmem_limit_bytes=40 * 2**20),
        name="residual",
    )(parent, basis, part, other)


def body(bounds, block_map, pivot_inverse, upper_block, lower_block, trailing_block, sketch, basis):
    me, row = lax.axis_index("front"), lax.axis_index("row")
    blocks = block_map.shape[1]
    per = basis.shape[1] // BLOCK
    per_front = per * lax.axis_size("row")
    boundary = bounds[0]
    entries = block_map.reshape(-1)
    order = jnp.arange(blocks, dtype=jnp.int32)
    slots = jnp.arange(FRONTS, dtype=jnp.int32)
    live = (row * blocks + order) * BLOCK < boundary

    dest = entries // per_front
    slot = jnp.where(live, slot_of(dest, me), FRONTS + order)
    place = jnp.sum((slot[None, :] < slot[:, None]).astype(jnp.int32), axis=1)
    at = (place[None, :] == order[:, None]).astype(jnp.int32)
    block_at = jnp.sum(at * order[None, :], axis=1)
    turned = jnp.sum(at * ((dest + me) % 2)[None, :], axis=1)
    place_of = jnp.sum(jnp.where(slot[None, :] == slots[:, None], place[None, :], 0), axis=1)
    tab = jnp.concatenate([bounds, block_at, turned, place_of])
    tag = jnp.sum(
        jnp.where(slot[None, :] == slots[:, None], (entries % per - per)[None, :], 0), axis=1
    ) + per
    tile = jnp.broadcast_to(jnp.pad(tag, (0, 128 - FRONTS))[None, :], (8, 128))

    land, marks = sketch_call(
        tab, tile, sketch, upper_block[0], pivot_inverse[0], lower_block[0], trailing_block[0]
    )
    tags = jnp.sum(
        jnp.where(jnp.arange(128, dtype=jnp.int32)[None, :] == slots[:, None], marks[:, 0, :], 0), axis=1
    )
    parent, part = parent_call(tags, land, basis[0])
    other = lax.ppermute(part, "row", [(0, 1), (1, 0)])
    residual, coefficients = residual_call(
        parent.reshape(per * BLOCK, -1), basis[0], part, other
    )
    return coefficients[None], residual[None]


def solution(mesh):
    placed = (
        P("front"),
        P("front", "row"),
        P("front", "col", "row"),
        P("front", "row", "col"),
        P("front", "row", "col"),
        P("front", "row", "col"),
        P("col", None),
        P("front", "row", None),
    )
    return jax.shard_map(
        body,
        mesh=mesh,
        in_specs=placed,
        out_specs=(P("front", None, "col"), P("front", "row", "col")),
        check_vma=False,
    )
```

```python
import jax
import jax.numpy as jnp
from jax import lax
from jax.experimental import pallas as pl
from jax.experimental.pallas import tpu as pltpu
from jax.sharding import PartitionSpec as P

BLOCK = 128
MESH = pl.DeviceIdType.MESH
F32 = jnp.float32
BF16 = jnp.bfloat16
FRONTS = 32
ORDER = (
    (2, 2, 1), (2, 2, 0), (2, 1, 1), (1, 2, 1), (2, 3, 0), (2, 3, 1), (3, 2, 1), (1, 2, 0), (1, 1, 1), (3, 3, 1),
    (2, 1, 0), (1, 3, 1), (3, 1, 1), (3, 2, 0), (0, 2, 1), (2, 0, 1), (0, 2, 0), (0, 3, 1), (1, 0, 1), (2, 0, 0),
    (3, 0, 1), (1, 1, 0), (3, 3, 0), (0, 1, 1), (1, 3, 0), (3, 1, 0), (0, 0, 1), (0, 1, 0), (1, 0, 0), (0, 3, 0),
    (3, 0, 0), (0, 0, 0),
)
HERE = FRONTS - 1


def slot_of(dest, source):
    (z, y, x), (sz, sy, sx) = ((f >> 3, (f >> 1) & 3, f & 1) for f in (dest, source))
    offset = (((z - sz) & 3) << 3) + (((y - sy) & 3) << 1) + (x ^ sx)
    codes = jnp.asarray([dz * 8 + dy * 2 + dx for dz, dy, dx in ORDER], jnp.int32)
    slots = jnp.arange(FRONTS, dtype=jnp.int32)
    return jnp.sum(jnp.where(offset[:, None] == codes[None, :], slots[None, :], 0), axis=1)


def sketch_kernel(
    tab, tile,
    sk_hbm, up_hbm, pi_hbm, lo_hbm, tr_hbm,
    land, marks,
    sk, up, pi, lo, tr, total, uown, usend, urecv, piv, vown, vrecv, solved, keep, pay, precv, summed, sbuf,
    ld, us, ur, vs, vr, ps, pr, ss, sr, ms, mr,
):
    me, row, col = lax.axis_index("front"), lax.axis_index("row"), lax.axis_index("col")
    blocks = total.shape[0]
    mate = {"col": 1 - col}
    twin = {"row": 1 - row}

    depth, width = me // 8, (me // 2) % 4
    depths = [((depth + d) % 4) * 8 for d in range(4)]
    widths = [((width + d) % 4) * 2 for d in range(4)]
    near = [me % 2, 1 - me % 2]
    cols = [col, 1 - col]
    others = [slot for slot in range(FRONTS) if slot != HERE]

    def peer(slot):
        dz, dy, dx = ORDER[slot]
        return {"front": depths[dz] + widths[dy] + near[dx], "col": cols[dx]}

    loads = [
        pltpu.make_async_copy(sk_hbm, sk, ld.at[0]),
        pltpu.make_async_copy(up_hbm, up, ld.at[1]),
        pltpu.make_async_copy(pi_hbm, pi, ld.at[2]),
    ]
    tiles = tr.shape[0]
    for t in range(tiles):
        loads.append(pltpu.make_async_copy(tr_hbm.at[t], tr.at[t], ld.at[3 + t]))
    loads.append(pltpu.make_async_copy(lo_hbm, lo, ld.at[3 + tiles]))
    for copy in loads:
        copy.start()

    barrier = pltpu.get_barrier_semaphore()
    pl.semaphore_signal(barrier, inc=1, device_id=mate, device_id_type=MESH)
    pl.semaphore_signal(barrier, inc=1, device_id=twin, device_id_type=MESH)

    for slot in others:
        pl.semaphore_signal(barrier, inc=1, device_id=peer(slot), device_id_type=MESH)

    loads[0].wait()
    height = sk.shape[0]
    bound = tab[0]
    step = 512

    @pl.loop(0, height // step)
    def _(i):
        at = pl.ds(pl.multiple_of(i * step, step), step)
        places = lax.broadcasted_iota(jnp.int32, (step, sk.shape[1]), 0) + (col * height + i * step)
        sk[at, :] = jnp.where(places < bound, sk[at, :].astype(F32), 0.0).astype(BF16)

    half = sk.shape[1] // 2
    loads[1].wait()
    usends = []
    for j in range(2):
        uown[j] = jnp.dot(up[...], sk[:, j * half : (j + 1) * half], preferred_element_type=F32)
        usend[j] = uown[j].astype(BF16)
        if j == 0:
            pl.semaphore_wait(barrier, FRONTS + 1)
        copy = pltpu.make_async_remote_copy(
            src_ref=usend.at[j], dst_ref=urecv.at[j], send_sem=us.at[j], recv_sem=ur.at[j],
            device_id=mate, device_id_type=MESH,
        )
        copy.start()
        usends.append(copy)

    def mark(slot):
        return pltpu.make_async_remote_copy(
            src_ref=tile, dst_ref=marks.at[slot], send_sem=ms.at[slot], recv_sem=mr.at[slot],
            device_id=peer(slot), device_id_type=MESH,
        )

    own_mark = pltpu.make_async_copy(tile, marks.at[HERE], ms.at[HERE])
    own_mark.start()
    for slot in others:
        mark(slot).start()

    per = blocks // tiles
    for t in range(tiles):
        loads[3 + t].wait()
        part = jnp.dot(tr[t], sk[...], preferred_element_type=F32)
        total[t * per : (t + 1) * per] = part.reshape(per, BLOCK, 2 * half)

    loads[2].wait()
    loads[3 + tiles].wait()
    vsends = []
    for j in range(2):
        usends[j].wait_recv()
        piv[...] = (uown[j] + urecv[j].astype(F32)).astype(BF16)
        vown[j] = jnp.dot(pi[...], piv[...], preferred_element_type=F32)
        copy = pltpu.make_async_remote_copy(
            src_ref=vown.at[j], dst_ref=vrecv.at[j], send_sem=vs.at[j], recv_sem=vr.at[j],
            device_id=twin, device_id_type=MESH,
        )
        copy.start()
        vsends.append(copy)
    for j in range(2):
        vsends[j].wait_recv()
        solved[:, j * half : (j + 1) * half] = (vown[j] + vrecv[j]).astype(BF16)

    def to_mate(p):
        return pltpu.make_async_remote_copy(
            src_ref=pay.at[p], dst_ref=precv.at[p], send_sem=ps.at[p], recv_sem=pr.at[p],
            device_id=mate, device_id_type=MESH,
        )

    def to_owner(slot):
        return pltpu.make_async_remote_copy(
            src_ref=sbuf.at[slot], dst_ref=land.at[slot], send_sem=ss.at[slot], recv_sem=sr.at[slot],
            device_id=peer(slot), device_id_type=MESH,
        )

    @pl.loop(0, blocks)
    def _(p):
        block = tab[1 + p]
        front = total[block] - jnp.dot(lo[block], solved[...], preferred_element_type=F32)
        left, right = front[:, :half], front[:, half:]
        stays = jnp.broadcast_to((tab[1 + blocks + p] + col) % 2, left.shape) == 0
        keep[p] = jnp.where(stays, left, right)
        pay[p] = jnp.where(stays, right, left).astype(BF16)
        to_mate(p).start()

    def fill(slot):
        sbuf[slot] = summed[tab[1 + 2 * blocks + slot]]

    def add(p):
        to_mate(p).wait_recv()
        summed[p] = (keep[p] + precv[p].astype(F32)).astype(BF16)
        fill(p)

    own = pltpu.make_async_copy(sbuf.at[HERE], land.at[HERE], ss.at[HERE])
    for slot in range(FRONTS):
        if slot < blocks:
            add(slot)
        else:
            fill(slot)
        if slot == HERE:
            own.start()
        else:
            to_owner(slot).start()

    for j in range(2):
        usends[j].wait_send()
        vsends[j].wait_send()

    @pl.loop(0, blocks)
    def _(p):
        to_mate(p).wait_send()

    own.wait()
    own_mark.wait()

    for slot in others:
        to_owner(slot).wait()
        mark(slot).wait()


def sketch_call(tab, tile, sketch, upper, pinv, lower, trailing):
    height, width = sketch.shape
    blocks = lower.shape[0] // BLOCK
    pivot = pinv.shape[0]
    half = width // 2
    tiles = 5
    hbm = pl.BlockSpec(memory_space=pltpu.HBM)
    vmem = pl.BlockSpec(memory_space=pltpu.VMEM)
    return pl.pallas_call(
        sketch_kernel,
        out_shape=(
            jax.ShapeDtypeStruct((FRONTS, BLOCK, half), BF16),
            jax.ShapeDtypeStruct((FRONTS,) + tile.shape, jnp.int32),
        ),
        in_specs=[pl.BlockSpec(memory_space=pltpu.SMEM), vmem] + [hbm] * 5,
        out_specs=(vmem, vmem),
        scratch_shapes=[
            pltpu.VMEM((height, width), BF16),
            pltpu.VMEM(upper.shape, BF16),
            pltpu.VMEM(pinv.shape, BF16),
            pltpu.VMEM((blocks, BLOCK, pivot), BF16),
            pltpu.VMEM((tiles, trailing.shape[0] // tiles, height), BF16),
            pltpu.VMEM((blocks, BLOCK, width), F32),
            pltpu.VMEM((2, pivot, half), F32),
            pltpu.VMEM((2, pivot, half), BF16),
            pltpu.VMEM((2, pivot, half), BF16),
            pltpu.VMEM((pivot, half), BF16),
            pltpu.VMEM((2, pivot, half), F32),
            pltpu.VMEM((2, pivot, half), F32),
            pltpu.VMEM((pivot, width), BF16),
            pltpu.VMEM((blocks, BLOCK, half), F32),
            pltpu.VMEM((blocks, BLOCK, half), BF16),
            pltpu.VMEM((blocks, BLOCK, half), BF16),
            pltpu.VMEM((blocks, BLOCK, half), BF16),
            pltpu.VMEM((FRONTS, BLOCK, half), BF16),
            pltpu.SemaphoreType.DMA((4 + tiles,)),
            pltpu.SemaphoreType.DMA((2,)),
            pltpu.SemaphoreType.DMA((2,)),
            pltpu.SemaphoreType.DMA((2,)),
            pltpu.SemaphoreType.DMA((2,)),
            pltpu.SemaphoreType.DMA((blocks,)),
            pltpu.SemaphoreType.DMA((blocks,)),
            pltpu.SemaphoreType.DMA((FRONTS,)),
            pltpu.SemaphoreType.DMA((FRONTS,)),
            pltpu.SemaphoreType.DMA((FRONTS,)),
            pltpu.SemaphoreType.DMA((FRONTS,)),
        ],
        compiler_params=pltpu.CompilerParams(
            collective_id=0, has_side_effects=True, vmem_limit_bytes=50 * 2**20
        ),
        cost_estimate=pl.CostEstimate(flops=10_000_000_000, bytes_accessed=100_000_000, transcendentals=0),
        name="sketch",
    )(
        tab, tile, sketch, upper, pinv,
        lower.reshape(blocks, BLOCK, pivot),
        trailing.reshape(tiles, trailing.shape[0] // tiles, height),
    )


def parent_kernel(tags, land, basis, parent, coeff):
    parent[...] = jnp.zeros_like(parent)
    per = parent.shape[0]

    @pl.loop(0, FRONTS)
    def _(slot):
        tag = tags[slot]

        @pl.when(tag < per)
        def _():
            parent[tag] += land[slot].astype(F32)

    rounded = parent[...].astype(BF16).reshape(per * BLOCK, parent.shape[2])
    coeff[...] = lax.dot_general(
        basis[...], rounded, (((0,), (0,)), ((), ())), preferred_element_type=F32
    )


def parent_call(tags, land, basis):
    rows, rank = basis.shape
    half = land.shape[2]
    vmem = pl.BlockSpec(memory_space=pltpu.VMEM)
    return pl.pallas_call(
        parent_kernel,
        out_shape=(
            jax.ShapeDtypeStruct((rows // BLOCK, BLOCK, half), F32),
            jax.ShapeDtypeStruct((rank, half), F32),
        ),
        in_specs=[pl.BlockSpec(memory_space=pltpu.SMEM), vmem, vmem],
        out_specs=(vmem, vmem),
        compiler_params=pltpu.CompilerParams(vmem_limit_bytes=40 * 2**20),
        name="parent",
    )(tags, land, basis)


def residual_kernel(parent, basis, part, other, out, coeff, tile, sems):
    total = part[...] + other[...]
    coeff[...] = total
    rounded = total.astype(BF16)
    rows = tile.shape[1]
    copies = []
    for i in range(parent.shape[0] // rows):
        if i >= 2:
            copies[i - 2].wait()
        at = pl.ds(i * rows, rows)
        tile[i % 2] = parent[at, :] - jnp.dot(basis[at, :], rounded, preferred_element_type=F32)
        copy = pltpu.make_async_copy(tile.at[i % 2], out.at[at, :], sems.at[i % 2])
        copy.start()
        copies.append(copy)
    copies[-2].wait()
    copies[-1].wait()


def residual_call(parent, basis, part, other):
    rows, rank = basis.shape
    half = parent.shape[1]
    vmem = pl.BlockSpec(memory_space=pltpu.VMEM)
    return pl.pallas_call(
        residual_kernel,
        out_shape=(
            jax.ShapeDtypeStruct((rows, half), F32),
            jax.ShapeDtypeStruct((rank, half), F32),
        ),
        in_specs=[vmem] * 4,
        out_specs=(pl.BlockSpec(memory_space=pltpu.HBM), vmem),
        scratch_shapes=[pltpu.VMEM((2, 512, half), F32), pltpu.SemaphoreType.DMA((2,))],
        compiler_params=pltpu.CompilerParams(vmem_limit_bytes=40 * 2**20),
        name="residual",
    )(parent, basis, part, other)


def body(bounds, block_map, pivot_inverse, upper_block, lower_block, trailing_block, sketch, basis):
    me, row = lax.axis_index("front"), lax.axis_index("row")
    blocks = block_map.shape[1]
    per = basis.shape[1] // BLOCK
    per_front = per * lax.axis_size("row")
    boundary = bounds[0]
    entries = block_map.reshape(-1)
    order = jnp.arange(blocks, dtype=jnp.int32)
    slots = jnp.arange(FRONTS, dtype=jnp.int32)
    live = (row * blocks + order) * BLOCK < boundary

    dest = entries // per_front
    slot = jnp.where(live, slot_of(dest, me), FRONTS + order)
    place = jnp.sum((slot[None, :] < slot[:, None]).astype(jnp.int32), axis=1)
    at = (place[None, :] == order[:, None]).astype(jnp.int32)
    block_at = jnp.sum(at * order[None, :], axis=1)
    turned = jnp.sum(at * ((dest + me) % 2)[None, :], axis=1)
    place_of = jnp.sum(jnp.where(slot[None, :] == slots[:, None], place[None, :], 0), axis=1)
    tab = jnp.concatenate([bounds, block_at, turned, place_of])
    tag = jnp.sum(
        jnp.where(slot[None, :] == slots[:, None], (entries % per - per)[None, :], 0), axis=1
    ) + per
    tile = jnp.broadcast_to(jnp.pad(tag, (0, 128 - FRONTS))[None, :], (8, 128))

    land, marks = sketch_call(
        tab, tile, sketch, upper_block[0], pivot_inverse[0], lower_block[0], trailing_block[0]
    )
    tags = jnp.sum(
        jnp.where(jnp.arange(128, dtype=jnp.int32)[None, :] == slots[:, None], marks[:, 0, :], 0), axis=1
    )
    parent, part = parent_call(tags, land, basis[0])
    other = lax.ppermute(part, "row", [(0, 1), (1, 0)])
    residual, coefficients = residual_call(
        parent.reshape(per * BLOCK, -1), basis[0], part, other
    )
    return coefficients[None], residual[None]


def solution(mesh):
    placed = (
        P("front"),
        P("front", "row"),
        P("front", "col", "row"),
        P("front", "row", "col"),
        P("front", "row", "col"),
        P("front", "row", "col"),
        P("col", None),
        P("front", "row", None),
    )
    return jax.shard_map(
        body,
        mesh=mesh,
        in_specs=placed,
        out_specs=(P("front", None, "col"), P("front", "row", "col")),
        check_vma=False,
    )
```

```python
import jax
import jax.numpy as jnp
from jax import lax
from jax.experimental import pallas as pl
from jax.experimental.pallas import tpu as pltpu
from jax.sharding import PartitionSpec as P

BLOCK = 128
MESH = pl.DeviceIdType.MESH
F32 = jnp.float32
BF16 = jnp.bfloat16
FRONTS = 32
ORDER = (
    (2, 2, 1), (2, 2, 0), (2, 1, 1), (1, 2, 1), (2, 3, 0), (2, 3, 1), (3, 2, 1), (1, 2, 0), (1, 1, 1), (3, 3, 1),
    (2, 1, 0), (1, 3, 1), (3, 1, 1), (3, 2, 0), (0, 2, 1), (2, 0, 1), (0, 2, 0), (0, 3, 1), (1, 0, 1), (2, 0, 0),
    (3, 0, 1), (1, 1, 0), (3, 3, 0), (0, 1, 1), (1, 3, 0), (3, 1, 0), (0, 0, 1), (0, 1, 0), (1, 0, 0), (0, 3, 0),
    (3, 0, 0), (0, 0, 0),
)
HERE = FRONTS - 1
EARLY = 4


def slot_of(dest, source):
    (z, y, x), (sz, sy, sx) = ((f >> 3, (f >> 1) & 3, f & 1) for f in (dest, source))
    offset = (((z - sz) & 3) << 3) + (((y - sy) & 3) << 1) + (x ^ sx)
    codes = jnp.asarray([dz * 8 + dy * 2 + dx for dz, dy, dx in ORDER], jnp.int32)
    slots = jnp.arange(FRONTS, dtype=jnp.int32)
    return jnp.sum(jnp.where(offset[:, None] == codes[None, :], slots[None, :], 0), axis=1)


def sketch_kernel(
    tab, tile,
    sk_hbm, up_hbm, pi_hbm, lo_hbm, tr_hbm,
    land, marks,
    sk, up, pi, lo, tr, total, uown, usend, urecv, piv, vown, vrecv, solved, keep, pay, precv, summed, sbuf,
    ld, us, ur, vs, vr, ps, pr, ss, sr, ms, mr,
):
    me, row, col = lax.axis_index("front"), lax.axis_index("row"), lax.axis_index("col")
    blocks = total.shape[0]
    mate = {"col": 1 - col}
    twin = {"row": 1 - row}

    depth, width = me // 8, (me // 2) % 4
    depths = [((depth + d) % 4) * 8 for d in range(4)]
    widths = [((width + d) % 4) * 2 for d in range(4)]
    near = [me % 2, 1 - me % 2]
    cols = [col, 1 - col]
    others = [slot for slot in range(FRONTS) if slot != HERE]

    def peer(slot):
        dz, dy, dx = ORDER[slot]
        return {"front": depths[dz] + widths[dy] + near[dx], "col": cols[dx]}

    loads = [
        pltpu.make_async_copy(up_hbm, up, ld.at[0]),
        pltpu.make_async_copy(pi_hbm, pi, ld.at[1]),
    ]
    quarter = sk.shape[1] // 4
    tiles = tr.shape[0]
    columns = [
        pltpu.make_async_copy(
            sk_hbm.at[:, pl.ds(q * quarter, quarter)], sk.at[:, pl.ds(i * quarter, quarter)], ld.at[3 + tiles + i]
        )
        for i, q in enumerate((0, 2, 1, 3))
    ]
    for copy in columns:
        copy.start()
    for t in range(tiles):
        loads.append(pltpu.make_async_copy(tr_hbm.at[t], tr.at[t], ld.at[2 + t]))
    loads.append(pltpu.make_async_copy(lo_hbm, lo, ld.at[2 + tiles]))
    for copy in loads:
        copy.start()

    barrier = pltpu.get_barrier_semaphore()
    pl.semaphore_signal(barrier, inc=1, device_id=mate, device_id_type=MESH)
    pl.semaphore_signal(barrier, inc=1, device_id=twin, device_id_type=MESH)

    for slot in others:
        pl.semaphore_signal(barrier, inc=1, device_id=peer(slot), device_id_type=MESH)

    for copy in columns:
        copy.wait()
    height = sk.shape[0]
    bound = tab[0]
    step = 512

    @pl.loop(0, height // step)
    def _(i):
        at = pl.ds(pl.multiple_of(i * step, step), step)
        places = lax.broadcasted_iota(jnp.int32, (step, sk.shape[1]), 0) + (col * height + i * step)
        sk[at, :] = jnp.where(places < bound, sk[at, :].astype(F32), 0.0).astype(BF16)

    half = sk.shape[1] // 2
    loads[0].wait()
    usends = []
    depth = up.shape[0] // 2
    for j in range(2):
        for h in range(2):
            at = pl.ds(h * depth, depth)
            uown[j, at, :] = jnp.dot(up[at, :], sk[:, j * half : (j + 1) * half], preferred_element_type=F32)
            usend[j, at, :] = uown[j, at, :].astype(BF16)
            if not usends:
                pl.semaphore_wait(barrier, FRONTS + 1)
            copy = pltpu.make_async_remote_copy(
                src_ref=usend.at[j, at], dst_ref=urecv.at[j, at], send_sem=us.at[2 * j + h], recv_sem=ur.at[2 * j + h],
                device_id=mate, device_id_type=MESH,
            )
            copy.start()
            usends.append(copy)

    def mark(slot):
        return pltpu.make_async_remote_copy(
            src_ref=tile, dst_ref=marks.at[slot], send_sem=ms.at[slot], recv_sem=mr.at[slot],
            device_id=peer(slot), device_id_type=MESH,
        )

    own_mark = pltpu.make_async_copy(tile, marks.at[HERE], ms.at[HERE])
    own_mark.start()
    for slot in others:
        mark(slot).start()

    per = blocks // tiles
    for t in range(tiles):
        loads[2 + t].wait()
        part = jnp.dot(tr[t], sk[...], preferred_element_type=F32)
        total[t * per : (t + 1) * per] = part.reshape(per, BLOCK, 2 * half)

    loads[1].wait()
    loads[2 + tiles].wait()

    def part_of(p, t):
        return pltpu.make_async_remote_copy(
            src_ref=pay.at[p, t], dst_ref=precv.at[p, t], send_sem=ps.at[p, t], recv_sem=pr.at[p, t],
            device_id=mate, device_id_type=MESH,
        )

    def to_mate(p):
        return pltpu.make_async_remote_copy(
            src_ref=pay.at[p], dst_ref=precv.at[p], send_sem=ps.at[p, 0], recv_sem=pr.at[p, 0],
            device_id=mate, device_id_type=MESH,
        )

    def put(p, front, t):
        left, right = front[:, :quarter], front[:, quarter:]
        stays = jnp.broadcast_to((tab[1 + blocks + p] + col) % 2, left.shape) == 0
        keep[p, :, t * quarter : (t + 1) * quarter] = jnp.where(stays, left, right)
        pay[p, t] = jnp.where(stays, right, left).astype(BF16)

    def half_front(p, t):
        block = tab[1 + p]
        at = slice(t * half, (t + 1) * half)
        return total[block, :, at] - jnp.dot(lo[block], solved[:, at], preferred_element_type=F32)

    vsends = []

    def solve(j):
        piv[...] = (uown[j] + urecv[j].astype(F32)).astype(BF16)
        vown[j] = jnp.dot(pi[...], piv[...], preferred_element_type=F32)
        copy = pltpu.make_async_remote_copy(
            src_ref=vown.at[j], dst_ref=vrecv.at[j], send_sem=vs.at[j], recv_sem=vr.at[j],
            device_id=twin, device_id_type=MESH,
        )
        copy.start()
        vsends.append(copy)

    def settle(j):
        vsends[j].wait_recv()
        solved[:, j * half : (j + 1) * half] = (vown[j] + vrecv[j]).astype(BF16)

    usends[0].wait_recv()
    usends[1].wait_recv()
    solve(0)
    settle(0)
    for p in range(EARLY):
        put(p, half_front(p, 0), 0)
    usends[2].wait_recv()
    usends[3].wait_recv()
    for p in range(EARLY):
        part_of(p, 0).start()
    solve(1)
    settle(1)
    for p in range(EARLY):
        put(p, half_front(p, 1), 1)
        part_of(p, 1).start()

    @pl.loop(EARLY, blocks)
    def _(p):
        block = tab[1 + p]
        front = total[block] - jnp.dot(lo[block], solved[...], preferred_element_type=F32)
        put(p, front[:, :half], 0)
        put(p, front[:, half:], 1)
        to_mate(p).start()

    def to_owner(slot):
        return pltpu.make_async_remote_copy(
            src_ref=sbuf.at[slot], dst_ref=land.at[slot], send_sem=ss.at[slot], recv_sem=sr.at[slot],
            device_id=peer(slot), device_id_type=MESH,
        )

    def fill(slot):
        sbuf[slot] = summed[tab[1 + 2 * blocks + slot]]

    def add(p):
        if p < EARLY:
            part_of(p, 0).wait_recv()
            part_of(p, 1).wait_recv()
        else:
            to_mate(p).wait_recv()
        for t in range(2):
            at = slice(t * quarter, (t + 1) * quarter)
            summed[p, :, at] = (keep[p, :, at] + precv[p, t].astype(F32)).astype(BF16)
        fill(p)

    own = pltpu.make_async_copy(sbuf.at[HERE], land.at[HERE], ss.at[HERE])
    for slot in range(FRONTS):
        if slot < blocks:
            add(slot)
        else:
            fill(slot)
        if slot == HERE:
            own.start()
        else:
            to_owner(slot).start()

    for copy in usends + vsends:
        copy.wait_send()
    for p in range(EARLY):
        part_of(p, 0).wait_send()
        part_of(p, 1).wait_send()

    @pl.loop(EARLY, blocks)
    def _(p):
        to_mate(p).wait_send()

    own.wait()
    own_mark.wait()

    for slot in others:
        to_owner(slot).wait()
        mark(slot).wait()


def sketch_call(tab, tile, sketch, upper, pinv, lower, trailing):
    height, width = sketch.shape
    blocks = lower.shape[0] // BLOCK
    pivot = pinv.shape[0]
    half = width // 2
    tiles = 5
    hbm = pl.BlockSpec(memory_space=pltpu.HBM)
    vmem = pl.BlockSpec(memory_space=pltpu.VMEM)
    return pl.pallas_call(
        sketch_kernel,
        out_shape=(
            jax.ShapeDtypeStruct((FRONTS, BLOCK, half), BF16),
            jax.ShapeDtypeStruct((FRONTS,) + tile.shape, jnp.int32),
        ),
        in_specs=[pl.BlockSpec(memory_space=pltpu.SMEM), vmem] + [hbm] * 5,
        out_specs=(vmem, vmem),
        scratch_shapes=[
            pltpu.VMEM((height, width), BF16),
            pltpu.VMEM(upper.shape, BF16),
            pltpu.VMEM(pinv.shape, BF16),
            pltpu.VMEM((blocks, BLOCK, pivot), BF16),
            pltpu.VMEM((tiles, trailing.shape[0] // tiles, height), BF16),
            pltpu.VMEM((blocks, BLOCK, width), F32),
            pltpu.VMEM((2, pivot, half), F32),
            pltpu.VMEM((2, pivot, half), BF16),
            pltpu.VMEM((2, pivot, half), BF16),
            pltpu.VMEM((pivot, half), BF16),
            pltpu.VMEM((2, pivot, half), F32),
            pltpu.VMEM((2, pivot, half), F32),
            pltpu.VMEM((pivot, width), BF16),
            pltpu.VMEM((blocks, BLOCK, half), F32),
            pltpu.VMEM((blocks, 2, BLOCK, half // 2), BF16),
            pltpu.VMEM((blocks, 2, BLOCK, half // 2), BF16),
            pltpu.VMEM((blocks, BLOCK, half), BF16),
            pltpu.VMEM((FRONTS, BLOCK, half), BF16),
            pltpu.SemaphoreType.DMA((8 + tiles,)),
            pltpu.SemaphoreType.DMA((4,)),
            pltpu.SemaphoreType.DMA((4,)),
            pltpu.SemaphoreType.DMA((2,)),
            pltpu.SemaphoreType.DMA((2,)),
            pltpu.SemaphoreType.DMA((blocks, 2)),
            pltpu.SemaphoreType.DMA((blocks, 2)),
            pltpu.SemaphoreType.DMA((FRONTS,)),
            pltpu.SemaphoreType.DMA((FRONTS,)),
            pltpu.SemaphoreType.DMA((FRONTS,)),
            pltpu.SemaphoreType.DMA((FRONTS,)),
        ],
        compiler_params=pltpu.CompilerParams(
            collective_id=0, has_side_effects=True, vmem_limit_bytes=50 * 2**20
        ),
        cost_estimate=pl.CostEstimate(flops=10_000_000_000, bytes_accessed=100_000_000, transcendentals=0),
        name="sketch",
    )(
        tab, tile, sketch, upper, pinv,
        lower.reshape(blocks, BLOCK, pivot),
        trailing.reshape(tiles, trailing.shape[0] // tiles, height),
    )


def parent_kernel(tags, land, basis, parent, coeff):
    parent[...] = jnp.zeros_like(parent)
    per = parent.shape[0]

    @pl.loop(0, FRONTS)
    def _(slot):
        tag = tags[slot]

        @pl.when(tag < per)
        def _():
            parent[tag] += land[slot].astype(F32)

    rounded = parent[...].astype(BF16).reshape(per * BLOCK, parent.shape[2])
    coeff[...] = lax.dot_general(
        basis[...], rounded, (((0,), (0,)), ((), ())), preferred_element_type=F32
    )


def parent_call(tags, land, basis):
    rows, rank = basis.shape
    half = land.shape[2]
    vmem = pl.BlockSpec(memory_space=pltpu.VMEM)
    return pl.pallas_call(
        parent_kernel,
        out_shape=(
            jax.ShapeDtypeStruct((rows // BLOCK, BLOCK, half), F32),
            jax.ShapeDtypeStruct((rank, half), F32),
        ),
        in_specs=[pl.BlockSpec(memory_space=pltpu.SMEM), vmem, vmem],
        out_specs=(vmem, vmem),
        compiler_params=pltpu.CompilerParams(vmem_limit_bytes=40 * 2**20),
        name="parent",
    )(tags, land, basis)


def residual_kernel(parent, basis, part, other, out, coeff, tile, sems):
    total = part[...] + other[...]
    coeff[...] = total
    rounded = total.astype(BF16)
    rows = tile.shape[1]
    copies = []
    for i in range(tile.shape[0]):
        at = pl.ds(i * rows, rows)
        tile[i] = parent[at, :] - jnp.dot(basis[at, :], rounded, preferred_element_type=F32)
        copy = pltpu.make_async_copy(tile.at[i], out.at[at, :], sems.at[i])
        copy.start()
        copies.append(copy)
    for copy in copies:
        copy.wait()


def residual_call(parent, basis, part, other):
    rows, rank = basis.shape
    half = parent.shape[1]
    vmem = pl.BlockSpec(memory_space=pltpu.VMEM)
    return pl.pallas_call(
        residual_kernel,
        out_shape=(
            jax.ShapeDtypeStruct((rows, half), F32),
            jax.ShapeDtypeStruct((rank, half), F32),
        ),
        in_specs=[vmem] * 4,
        out_specs=(pl.BlockSpec(memory_space=pltpu.HBM), vmem),
        scratch_shapes=[pltpu.VMEM((rows // 512, 512, half), F32), pltpu.SemaphoreType.DMA((rows // 512,))],
        compiler_params=pltpu.CompilerParams(vmem_limit_bytes=24 * 2**20),
        name="residual",
    )(parent, basis, part, other)


def body(bounds, block_map, pivot_inverse, upper_block, lower_block, trailing_block, sketch, basis):
    me, row = lax.axis_index("front"), lax.axis_index("row")
    blocks = block_map.shape[1]
    per = basis.shape[1] // BLOCK
    per_front = per * lax.axis_size("row")
    boundary = bounds[0]
    entries = block_map.reshape(-1)
    order = jnp.arange(blocks, dtype=jnp.int32)
    slots = jnp.arange(FRONTS, dtype=jnp.int32)
    live = (row * blocks + order) * BLOCK < boundary

    dest = entries // per_front
    slot = jnp.where(live, slot_of(dest, me), FRONTS + order)
    place = jnp.sum((slot[None, :] < slot[:, None]).astype(jnp.int32), axis=1)
    at = (place[None, :] == order[:, None]).astype(jnp.int32)
    block_at = jnp.sum(at * order[None, :], axis=1)
    turned = jnp.sum(at * ((dest + me) % 2)[None, :], axis=1)
    place_of = jnp.sum(jnp.where(slot[None, :] == slots[:, None], place[None, :], 0), axis=1)
    tab = jnp.concatenate([bounds, block_at, turned, place_of])
    tag = jnp.sum(
        jnp.where(slot[None, :] == slots[:, None], (entries % per - per)[None, :], 0), axis=1
    ) + per
    tile = jnp.broadcast_to(jnp.pad(tag, (0, 128 - FRONTS))[None, :], (8, 128))

    land, marks = sketch_call(
        tab, tile, sketch, upper_block[0], pivot_inverse[0], lower_block[0], trailing_block[0]
    )
    tags = jnp.sum(
        jnp.where(jnp.arange(128, dtype=jnp.int32)[None, :] == slots[:, None], marks[:, 0, :], 0), axis=1
    )
    parent, part = parent_call(tags, land, basis[0])
    other = lax.ppermute(part, "row", [(0, 1), (1, 0)])
    residual, coefficients = residual_call(
        parent.reshape(per * BLOCK, -1), basis[0], part, other
    )
    return coefficients[None], residual[None]


def solution(mesh):
    placed = (
        P("front"),
        P("front", "row"),
        P("front", "col", "row"),
        P("front", "row", "col"),
        P("front", "row", "col"),
        P("front", "row", "col"),
        P("col", None),
        P("front", "row", None),
    )
    return jax.shard_map(
        body,
        mesh=mesh,
        in_specs=placed,
        out_specs=(P("front", None, "col"), P("front", "row", "col")),
        check_vma=False,
    )
```

```python
import functools

import jax
import jax.numpy as jnp
from jax import lax
from jax.experimental import pallas as pl
from jax.experimental.pallas import tpu as pltpu
from jax.sharding import PartitionSpec as P

BLOCK = 128
MESH = pl.DeviceIdType.MESH
F32 = jnp.float32
BF16 = jnp.bfloat16
FRONTS = 32
ORDER = (
    (2, 2, 1), (2, 2, 0), (2, 1, 1), (1, 2, 1), (2, 3, 0), (2, 3, 1), (3, 2, 1), (1, 2, 0), (1, 1, 1), (3, 3, 1),
    (2, 1, 0), (1, 3, 1), (3, 1, 1), (3, 2, 0), (0, 2, 1), (2, 0, 1), (0, 2, 0), (0, 3, 1), (1, 0, 1), (2, 0, 0),
    (3, 0, 1), (1, 1, 0), (3, 3, 0), (0, 1, 1), (1, 3, 0), (3, 1, 0), (0, 0, 1), (0, 1, 0), (1, 0, 0), (0, 3, 0),
    (3, 0, 0), (0, 0, 0),
)
HERE = FRONTS - 1
EARLY = 4


def total_over(values, axis):
    return jnp.sum(values, axis=axis, keepdims=True)


def tables_of(entries, bound, me, row, per):
    blocks = entries.shape[1]
    down = lax.broadcasted_iota(jnp.int32, (blocks, blocks), 0)
    along = lax.broadcasted_iota(jnp.int32, (blocks, blocks), 1)
    order = lax.broadcasted_iota(jnp.int32, (blocks, 1), 0)
    slots = lax.broadcasted_iota(jnp.int32, (blocks, FRONTS), 1)
    held = total_over(jnp.where(down == along, jnp.broadcast_to(entries, (blocks, blocks)), 0), 1)
    dest = total_over((held >= 2 * per * (slots + 1)).astype(jnp.int32), 1)
    depth, width, near = dest >> 3, (dest >> 1) & 3, dest & 1
    turned = (near + me % 2) & 1
    offset = (((depth - me // 8) & 3) << 3) + (((width - (me // 2) % 4) & 3) << 1) + turned
    slot = jnp.zeros_like(offset)
    for s, (dz, dy, dx) in enumerate(ORDER):
        slot = jnp.where(offset == dz * 8 + dy * 2 + dx, s, slot)
    slot = jnp.where((row * blocks + order) * BLOCK < bound, slot, FRONTS + order)
    wide = jnp.broadcast_to(slot, (blocks, blocks))
    slot_along = total_over(jnp.where(down == along, wide, 0), 0)
    place = total_over((slot_along < wide).astype(jnp.int32), 1)
    at = place == along
    hit = slot == slots
    rest = held - 2 * per * dest
    local = jnp.where(rest >= per, rest - per, rest)
    return (
        total_over(jnp.where(at, down, 0), 0),
        total_over(jnp.where(at, turned, 0), 0),
        total_over(jnp.where(hit, place, 0), 0),
        total_over(jnp.where(hit, local - per, 0), 0) + per,
    )


def sketch_kernel(
    per_device,
    bounds, block_map,
    sk_hbm, up_hbm, pi_hbm, lo_hbm, tr_hbm,
    land, marks,
    tile, tabv, tab, sk, up, pi, lo, tr, total, uown, usend, urecv, piv, vown, vrecv, solved, keep, pay, precv, summed, sbuf,
    ld, us, ur, vs, vr, ps, pr, ss, sr, ms, mr, ts,
):
    me, row, col = lax.axis_index("front"), lax.axis_index("row"), lax.axis_index("col")
    blocks = total.shape[0]
    mate = {"col": 1 - col}
    twin = {"row": 1 - row}

    depth, width = me // 8, (me // 2) % 4
    depths = [((depth + d) % 4) * 8 for d in range(4)]
    widths = [((width + d) % 4) * 2 for d in range(4)]
    near = [me % 2, 1 - me % 2]
    cols = [col, 1 - col]
    others = [slot for slot in range(FRONTS) if slot != HERE]

    def peer(slot):
        dz, dy, dx = ORDER[slot]
        return {"front": depths[dz] + widths[dy] + near[dx], "col": cols[dx]}

    loads = [
        pltpu.make_async_copy(up_hbm, up, ld.at[0]),
        pltpu.make_async_copy(pi_hbm, pi, ld.at[1]),
    ]
    quarter = sk.shape[1] // 4
    tiles = tr.shape[0]
    columns = [
        pltpu.make_async_copy(
            sk_hbm.at[:, pl.ds(q * quarter, quarter)], sk.at[:, pl.ds(i * quarter, quarter)], ld.at[3 + tiles + i]
        )
        for i, q in enumerate((0, 2, 1, 3))
    ]
    for copy in columns:
        copy.start()
    for t in range(tiles):
        loads.append(pltpu.make_async_copy(tr_hbm.at[t], tr.at[t], ld.at[2 + t]))
    loads.append(pltpu.make_async_copy(lo_hbm, lo, ld.at[2 + tiles]))
    for copy in loads:
        copy.start()

    barrier = pltpu.get_barrier_semaphore()
    pl.semaphore_signal(barrier, inc=1, device_id=mate, device_id_type=MESH)
    pl.semaphore_signal(barrier, inc=1, device_id=twin, device_id_type=MESH)

    for slot in others:
        pl.semaphore_signal(barrier, inc=1, device_id=peer(slot), device_id_type=MESH)

    for copy in columns:
        copy.wait()
    height = sk.shape[0]
    bound = bounds[0]
    step = 512

    @pl.loop(0, height // step)
    def _(i):
        at = pl.ds(pl.multiple_of(i * step, step), step)
        places = lax.broadcasted_iota(jnp.int32, (step, sk.shape[1]), 0) + (col * height + i * step)
        sk[at, :] = jnp.where(places < bound, sk[at, :].astype(F32), 0.0).astype(BF16)

    half = sk.shape[1] // 2
    loads[0].wait()
    usends = []
    depth = up.shape[0] // 2
    for j in range(2):
        for h in range(2):
            at = pl.ds(h * depth, depth)
            uown[j, at, :] = jnp.dot(up[at, :], sk[:, j * half : (j + 1) * half], preferred_element_type=F32)
            usend[j, at, :] = uown[j, at, :].astype(BF16)
            if not usends:
                pl.semaphore_wait(barrier, FRONTS + 1)
            copy = pltpu.make_async_remote_copy(
                src_ref=usend.at[j, at], dst_ref=urecv.at[j, at], send_sem=us.at[2 * j + h], recv_sem=ur.at[2 * j + h],
                device_id=mate, device_id_type=MESH,
            )
            copy.start()
            usends.append(copy)

    def mark(slot):
        return pltpu.make_async_remote_copy(
            src_ref=tile, dst_ref=marks.at[slot], send_sem=ms.at[slot], recv_sem=mr.at[slot],
            device_id=peer(slot), device_id_type=MESH,
        )

    rows_of = tables_of(block_map[...], bound, me, row, per_device)
    tile[...] = jnp.zeros_like(tile)
    tile[:, :FRONTS] = jnp.broadcast_to(rows_of[3], (tile.shape[0], FRONTS))
    tabv[...] = jnp.zeros_like(tabv)
    for i in range(3):
        tabv[i : i + 1, : rows_of[i].shape[1]] = rows_of[i]
    to_scalars = pltpu.make_async_copy(tabv, tab, ts)
    to_scalars.start()
    own_mark = pltpu.make_async_copy(tile, marks.at[HERE], ms.at[HERE])
    own_mark.start()
    for slot in others:
        mark(slot).start()

    per = blocks // tiles
    for t in range(tiles):
        loads[2 + t].wait()
        part = jnp.dot(tr[t], sk[...], preferred_element_type=F32)
        total[t * per : (t + 1) * per] = part.reshape(per, BLOCK, 2 * half)

    to_scalars.wait()
    loads[1].wait()
    loads[2 + tiles].wait()

    def part_of(p, t):
        return pltpu.make_async_remote_copy(
            src_ref=pay.at[p, t], dst_ref=precv.at[p, t], send_sem=ps.at[p, t], recv_sem=pr.at[p, t],
            device_id=mate, device_id_type=MESH,
        )

    def to_mate(p):
        return pltpu.make_async_remote_copy(
            src_ref=pay.at[p], dst_ref=precv.at[p], send_sem=ps.at[p, 0], recv_sem=pr.at[p, 0],
            device_id=mate, device_id_type=MESH,
        )

    def put(p, front, t):
        left, right = front[:, :quarter], front[:, quarter:]
        stays = jnp.broadcast_to((tab[1, p] + col) % 2, left.shape) == 0
        keep[p, :, t * quarter : (t + 1) * quarter] = jnp.where(stays, left, right)
        pay[p, t] = jnp.where(stays, right, left).astype(BF16)

    def half_front(p, t):
        block = tab[0, p]
        at = slice(t * half, (t + 1) * half)
        return total[block, :, at] - jnp.dot(lo[block], solved[:, at], preferred_element_type=F32)

    vsends = []

    def solve(j):
        piv[...] = (uown[j] + urecv[j].astype(F32)).astype(BF16)
        vown[j] = jnp.dot(pi[...], piv[...], preferred_element_type=F32)
        copy = pltpu.make_async_remote_copy(
            src_ref=vown.at[j], dst_ref=vrecv.at[j], send_sem=vs.at[j], recv_sem=vr.at[j],
            device_id=twin, device_id_type=MESH,
        )
        copy.start()
        vsends.append(copy)

    def settle(j):
        vsends[j].wait_recv()
        solved[:, j * half : (j + 1) * half] = (vown[j] + vrecv[j]).astype(BF16)

    usends[0].wait_recv()
    usends[1].wait_recv()
    solve(0)
    settle(0)
    for p in range(EARLY):
        put(p, half_front(p, 0), 0)
    usends[2].wait_recv()
    usends[3].wait_recv()
    for p in range(EARLY):
        part_of(p, 0).start()
    solve(1)
    settle(1)
    for p in range(EARLY):
        put(p, half_front(p, 1), 1)
        part_of(p, 1).start()

    @pl.loop(EARLY, blocks)
    def _(p):
        block = tab[0, p]
        front = total[block] - jnp.dot(lo[block], solved[...], preferred_element_type=F32)
        put(p, front[:, :half], 0)
        put(p, front[:, half:], 1)
        to_mate(p).start()

    def to_owner(slot):
        return pltpu.make_async_remote_copy(
            src_ref=sbuf.at[slot], dst_ref=land.at[slot], send_sem=ss.at[slot], recv_sem=sr.at[slot],
            device_id=peer(slot), device_id_type=MESH,
        )

    def fill(slot):
        sbuf[slot] = summed[tab[2, slot]]

    def add(p):
        if p < EARLY:
            part_of(p, 0).wait_recv()
            part_of(p, 1).wait_recv()
        else:
            to_mate(p).wait_recv()
        for t in range(2):
            at = slice(t * quarter, (t + 1) * quarter)
            summed[p, :, at] = (keep[p, :, at] + precv[p, t].astype(F32)).astype(BF16)
        fill(p)

    own = pltpu.make_async_copy(sbuf.at[HERE], land.at[HERE], ss.at[HERE])
    for slot in range(FRONTS):
        if slot < blocks:
            add(slot)
        else:
            fill(slot)
        if slot == HERE:
            own.start()
        else:
            to_owner(slot).start()

    for copy in usends + vsends:
        copy.wait_send()
    for p in range(EARLY):
        part_of(p, 0).wait_send()
        part_of(p, 1).wait_send()

    @pl.loop(EARLY, blocks)
    def _(p):
        to_mate(p).wait_send()

    own.wait()
    own_mark.wait()

    for slot in others:
        to_owner(slot).wait()
        mark(slot).wait()


def sketch_call(per_device, bounds, block_map, sketch, upper, pinv, lower, trailing):
    height, width = sketch.shape
    blocks = lower.shape[0] // BLOCK
    pivot = pinv.shape[0]
    half = width // 2
    tiles = 5
    hbm = pl.BlockSpec(memory_space=pltpu.HBM)
    vmem = pl.BlockSpec(memory_space=pltpu.VMEM)
    return pl.pallas_call(
        functools.partial(sketch_kernel, per_device),
        out_shape=(
            jax.ShapeDtypeStruct((FRONTS, BLOCK, half), BF16),
            jax.ShapeDtypeStruct((FRONTS, 8, 128), jnp.int32),
        ),
        in_specs=[pl.BlockSpec(memory_space=pltpu.SMEM), vmem] + [hbm] * 5,
        out_specs=(vmem, vmem),
        scratch_shapes=[
            pltpu.VMEM((8, 128), jnp.int32),
            pltpu.VMEM((8, 128), jnp.int32),
            pltpu.SMEM((8, 128), jnp.int32),
            pltpu.VMEM((height, width), BF16),
            pltpu.VMEM(upper.shape, BF16),
            pltpu.VMEM(pinv.shape, BF16),
            pltpu.VMEM((blocks, BLOCK, pivot), BF16),
            pltpu.VMEM((tiles, trailing.shape[0] // tiles, height), BF16),
            pltpu.VMEM((blocks, BLOCK, width), F32),
            pltpu.VMEM((2, pivot, half), F32),
            pltpu.VMEM((2, pivot, half), BF16),
            pltpu.VMEM((2, pivot, half), BF16),
            pltpu.VMEM((pivot, half), BF16),
            pltpu.VMEM((2, pivot, half), F32),
            pltpu.VMEM((2, pivot, half), F32),
            pltpu.VMEM((pivot, width), BF16),
            pltpu.VMEM((blocks, BLOCK, half), F32),
            pltpu.VMEM((blocks, 2, BLOCK, half // 2), BF16),
            pltpu.VMEM((blocks, 2, BLOCK, half // 2), BF16),
            pltpu.VMEM((blocks, BLOCK, half), BF16),
            pltpu.VMEM((FRONTS, BLOCK, half), BF16),
            pltpu.SemaphoreType.DMA((8 + tiles,)),
            pltpu.SemaphoreType.DMA((4,)),
            pltpu.SemaphoreType.DMA((4,)),
            pltpu.SemaphoreType.DMA((2,)),
            pltpu.SemaphoreType.DMA((2,)),
            pltpu.SemaphoreType.DMA((blocks, 2)),
            pltpu.SemaphoreType.DMA((blocks, 2)),
            pltpu.SemaphoreType.DMA((FRONTS,)),
            pltpu.SemaphoreType.DMA((FRONTS,)),
            pltpu.SemaphoreType.DMA((FRONTS,)),
            pltpu.SemaphoreType.DMA((FRONTS,)),
            pltpu.SemaphoreType.DMA,
        ],
        compiler_params=pltpu.CompilerParams(
            collective_id=0, has_side_effects=True, vmem_limit_bytes=50 * 2**20
        ),
        cost_estimate=pl.CostEstimate(flops=10_000_000_000, bytes_accessed=100_000_000, transcendentals=0),
        name="sketch",
    )(
        bounds, block_map, sketch, upper, pinv,
        lower.reshape(blocks, BLOCK, pivot),
        trailing.reshape(tiles, trailing.shape[0] // tiles, height),
    )


def parent_kernel(tags, land, basis, parent, coeff):
    parent[...] = jnp.zeros_like(parent)
    per = parent.shape[0]

    @pl.loop(0, FRONTS)
    def _(slot):
        tag = tags[slot]

        @pl.when(tag < per)
        def _():
            parent[tag] += land[slot].astype(F32)

    rounded = parent[...].astype(BF16).reshape(per * BLOCK, parent.shape[2])
    coeff[...] = lax.dot_general(
        basis[...], rounded, (((0,), (0,)), ((), ())), preferred_element_type=F32
    )


def parent_call(tags, land, basis):
    rows, rank = basis.shape
    half = land.shape[2]
    vmem = pl.BlockSpec(memory_space=pltpu.VMEM)
    return pl.pallas_call(
        parent_kernel,
        out_shape=(
            jax.ShapeDtypeStruct((rows // BLOCK, BLOCK, half), F32),
            jax.ShapeDtypeStruct((rank, half), F32),
        ),
        in_specs=[pl.BlockSpec(memory_space=pltpu.SMEM), vmem, vmem],
        out_specs=(vmem, vmem),
        compiler_params=pltpu.CompilerParams(vmem_limit_bytes=40 * 2**20),
        name="parent",
    )(tags, land, basis)


def residual_kernel(parent, basis, part, other, out, coeff, tile, sems):
    total = part[...] + other[...]
    coeff[...] = total
    rounded = total.astype(BF16)
    rows = tile.shape[1]
    copies = []
    for i in range(tile.shape[0]):
        at = pl.ds(i * rows, rows)
        tile[i] = parent[at, :] - jnp.dot(basis[at, :], rounded, preferred_element_type=F32)
        copy = pltpu.make_async_copy(tile.at[i], out.at[at, :], sems.at[i])
        copy.start()
        copies.append(copy)
    for copy in copies:
        copy.wait()


def residual_call(parent, basis, part, other):
    rows, rank = basis.shape
    half = parent.shape[1]
    vmem = pl.BlockSpec(memory_space=pltpu.VMEM)
    return pl.pallas_call(
        residual_kernel,
        out_shape=(
            jax.ShapeDtypeStruct((rows, half), F32),
            jax.ShapeDtypeStruct((rank, half), F32),
        ),
        in_specs=[vmem] * 4,
        out_specs=(pl.BlockSpec(memory_space=pltpu.HBM), vmem),
        scratch_shapes=[pltpu.VMEM((rows // 512, 512, half), F32), pltpu.SemaphoreType.DMA((rows // 512,))],
        compiler_params=pltpu.CompilerParams(vmem_limit_bytes=24 * 2**20),
        name="residual",
    )(parent, basis, part, other)


def body(bounds, block_map, pivot_inverse, upper_block, lower_block, trailing_block, sketch, basis):
    per = basis.shape[1] // BLOCK
    slots = jnp.arange(FRONTS, dtype=jnp.int32)
    land, marks = sketch_call(
        per, bounds, block_map, sketch, upper_block[0], pivot_inverse[0], lower_block[0], trailing_block[0]
    )
    tags = jnp.sum(
        jnp.where(jnp.arange(128, dtype=jnp.int32)[None, :] == slots[:, None], marks[:, 0, :], 0), axis=1
    )
    parent, part = parent_call(tags, land, basis[0])
    other = lax.ppermute(part, "row", [(0, 1), (1, 0)])
    residual, coefficients = residual_call(
        parent.reshape(per * BLOCK, -1), basis[0], part, other
    )
    return coefficients[None], residual[None]


def solution(mesh):
    placed = (
        P("front"),
        P("front", "row"),
        P("front", "col", "row"),
        P("front", "row", "col"),
        P("front", "row", "col"),
        P("front", "row", "col"),
        P("col", None),
        P("front", "row", None),
    )
    return jax.shard_map(
        body,
        mesh=mesh,
        in_specs=placed,
        out_specs=(P("front", None, "col"), P("front", "row", "col")),
        check_vma=False,
    )
```

```python
import functools

import jax
import jax.numpy as jnp
from jax import lax
from jax.experimental import pallas as pl
from jax.experimental.pallas import tpu as pltpu
from jax.sharding import PartitionSpec as P

BLOCK = 128
MESH = pl.DeviceIdType.MESH
F32 = jnp.float32
BF16 = jnp.bfloat16
FRONTS = 32
ORDER = (
    (2, 2, 1), (2, 2, 0), (2, 1, 1), (1, 2, 1), (2, 3, 0), (2, 3, 1), (3, 2, 1), (1, 2, 0), (1, 1, 1), (3, 3, 1),
    (2, 1, 0), (1, 3, 1), (3, 1, 1), (3, 2, 0), (0, 2, 1), (2, 0, 1), (0, 2, 0), (0, 3, 1), (1, 0, 1), (2, 0, 0),
    (3, 0, 1), (1, 1, 0), (3, 3, 0), (0, 1, 1), (1, 3, 0), (3, 1, 0), (0, 0, 1), (0, 1, 0), (1, 0, 0), (0, 3, 0),
    (3, 0, 0), (0, 0, 0),
)
HERE = FRONTS - 1
EARLY = 4


def total_over(values, axis):
    return jnp.sum(values, axis=axis, keepdims=True)


def tables_of(entries, bound, me, row, per):
    blocks = entries.shape[1]
    down = lax.broadcasted_iota(jnp.int32, (blocks, blocks), 0)
    along = lax.broadcasted_iota(jnp.int32, (blocks, blocks), 1)
    order = lax.broadcasted_iota(jnp.int32, (blocks, 1), 0)
    slots = lax.broadcasted_iota(jnp.int32, (blocks, FRONTS), 1)
    held = total_over(jnp.where(down == along, jnp.broadcast_to(entries, (blocks, blocks)), 0), 1)
    dest = total_over((held >= 2 * per * (slots + 1)).astype(jnp.int32), 1)
    depth, width, near = dest >> 3, (dest >> 1) & 3, dest & 1
    turned = (near + me % 2) & 1
    offset = (((depth - me // 8) & 3) << 3) + (((width - (me // 2) % 4) & 3) << 1) + turned
    slot = jnp.zeros_like(offset)
    for s, (dz, dy, dx) in enumerate(ORDER):
        slot = jnp.where(offset == dz * 8 + dy * 2 + dx, s, slot)
    slot = jnp.where((row * blocks + order) * BLOCK < bound, slot, FRONTS + order)
    wide = jnp.broadcast_to(slot, (blocks, blocks))
    slot_along = total_over(jnp.where(down == along, wide, 0), 0)
    place = total_over((slot_along < wide).astype(jnp.int32), 1)
    at = place == along
    hit = slot == slots
    rest = held - 2 * per * dest
    local = jnp.where(rest >= per, rest - per, rest)
    return (
        total_over(jnp.where(at, down, 0), 0),
        total_over(jnp.where(at, turned, 0), 0),
        total_over(jnp.where(hit, place, 0), 0),
        total_over(jnp.where(hit, local - per, 0), 0) + per,
    )


def sketch_kernel(
    per_device,
    bounds, block_map,
    sk_hbm, up_hbm, pi_hbm, lo_hbm, tr_hbm,
    land, marks,
    tile, tabv, tab, sk, up, pi, lo, tr, total, uown, usend, urecv, piv, vown, vrecv, solved, keep, pay, precv, summed, sbuf,
    ld, us, ur, vs, vr, ps, pr, ss, sr, ms, mr, ts,
):
    me, row, col = lax.axis_index("front"), lax.axis_index("row"), lax.axis_index("col")
    blocks = total.shape[0]
    mate = {"col": 1 - col}
    twin = {"row": 1 - row}

    depth, width = me // 8, (me // 2) % 4
    depths = [((depth + d) % 4) * 8 for d in range(4)]
    widths = [((width + d) % 4) * 2 for d in range(4)]
    near = [me % 2, 1 - me % 2]
    cols = [col, 1 - col]
    others = [slot for slot in range(FRONTS) if slot != HERE]

    def peer(slot):
        dz, dy, dx = ORDER[slot]
        return {"front": depths[dz] + widths[dy] + near[dx], "col": cols[dx]}

    loads = [
        pltpu.make_async_copy(up_hbm, up, ld.at[0]),
        pltpu.make_async_copy(pi_hbm, pi, ld.at[1]),
    ]
    quarter = sk.shape[1] // 4
    tiles = tr.shape[0]
    columns = [
        pltpu.make_async_copy(
            sk_hbm.at[:, pl.ds(q * quarter, quarter)], sk.at[:, pl.ds(i * quarter, quarter)], ld.at[3 + tiles + i]
        )
        for i, q in enumerate((0, 2, 1, 3))
    ]
    for copy in columns:
        copy.start()
    for t in range(tiles):
        loads.append(pltpu.make_async_copy(tr_hbm.at[t], tr.at[t], ld.at[2 + t]))
    loads.append(pltpu.make_async_copy(lo_hbm, lo, ld.at[2 + tiles]))
    for copy in loads:
        copy.start()

    barrier = pltpu.get_barrier_semaphore()
    pl.semaphore_signal(barrier, inc=1, device_id=mate, device_id_type=MESH)
    pl.semaphore_signal(barrier, inc=1, device_id=twin, device_id_type=MESH)

    for slot in others:
        pl.semaphore_signal(barrier, inc=1, device_id=peer(slot), device_id_type=MESH)

    for copy in columns:
        copy.wait()
    height = sk.shape[0]
    bound = bounds[0]
    step = 512

    @pl.loop(0, height // step)
    def _(i):
        at = pl.ds(pl.multiple_of(i * step, step), step)
        places = lax.broadcasted_iota(jnp.int32, (step, sk.shape[1]), 0) + (col * height + i * step)
        sk[at, :] = jnp.where(places < bound, sk[at, :].astype(F32), 0.0).astype(BF16)

    half = sk.shape[1] // 2
    loads[0].wait()
    usends = []
    depth = up.shape[0] // 2
    for j in range(2):
        for h in range(2):
            at = pl.ds(h * depth, depth)
            uown[j, at, :] = jnp.dot(up[at, :], sk[:, j * half : (j + 1) * half], preferred_element_type=F32)
            usend[j, at, :] = uown[j, at, :].astype(BF16)
            if not usends:
                pl.semaphore_wait(barrier, FRONTS + 1)
            copy = pltpu.make_async_remote_copy(
                src_ref=usend.at[j, at], dst_ref=urecv.at[j, at], send_sem=us.at[2 * j + h], recv_sem=ur.at[2 * j + h],
                device_id=mate, device_id_type=MESH,
            )
            copy.start()
            usends.append(copy)

    def mark(slot):
        return pltpu.make_async_remote_copy(
            src_ref=tile, dst_ref=marks.at[slot], send_sem=ms.at[slot], recv_sem=mr.at[slot],
            device_id=peer(slot), device_id_type=MESH,
        )

    rows_of = tables_of(block_map[...], bound, me, row, per_device)
    tile[...] = jnp.zeros_like(tile)
    tile[:, :FRONTS] = jnp.broadcast_to(rows_of[3], (tile.shape[0], FRONTS))
    tabv[...] = jnp.zeros_like(tabv)
    for i in range(3):
        tabv[i : i + 1, : rows_of[i].shape[1]] = rows_of[i]
    to_scalars = pltpu.make_async_copy(tabv, tab, ts)
    to_scalars.start()
    own_mark = pltpu.make_async_copy(tile, marks.at[HERE], ms.at[HERE])
    own_mark.start()
    for slot in others:
        mark(slot).start()

    per = blocks // tiles
    for t in range(tiles):
        loads[2 + t].wait()
        part = jnp.dot(tr[t], sk[...], preferred_element_type=F32)
        total[t * per : (t + 1) * per] = part.reshape(per, BLOCK, 2 * half)

    to_scalars.wait()
    loads[1].wait()
    loads[2 + tiles].wait()

    def part_of(p, t):
        return pltpu.make_async_remote_copy(
            src_ref=pay.at[p, t], dst_ref=precv.at[p, t], send_sem=ps.at[p, t], recv_sem=pr.at[p, t],
            device_id=mate, device_id_type=MESH,
        )

    def to_mate(p):
        return pltpu.make_async_remote_copy(
            src_ref=pay.at[p], dst_ref=precv.at[p], send_sem=ps.at[p, 0], recv_sem=pr.at[p, 0],
            device_id=mate, device_id_type=MESH,
        )

    def put(p, front, t):
        left, right = front[:, :quarter], front[:, quarter:]
        stays = jnp.broadcast_to((tab[1, p] + col) % 2, left.shape) == 0
        keep[p, :, t * quarter : (t + 1) * quarter] = jnp.where(stays, left, right)
        pay[p, t] = jnp.where(stays, right, left).astype(BF16)

    def half_front(p, t):
        block = tab[0, p]
        at = slice(t * half, (t + 1) * half)
        return total[block, :, at] - jnp.dot(lo[block], solved[:, at], preferred_element_type=F32)

    vsends = []

    def solve(j):
        piv[...] = (uown[j] + urecv[j].astype(F32)).astype(BF16)
        vown[j] = jnp.dot(pi[...], piv[...], preferred_element_type=F32)
        copy = pltpu.make_async_remote_copy(
            src_ref=vown.at[j], dst_ref=vrecv.at[j], send_sem=vs.at[j], recv_sem=vr.at[j],
            device_id=twin, device_id_type=MESH,
        )
        copy.start()
        vsends.append(copy)

    def settle(j):
        vsends[j].wait_recv()
        solved[:, j * half : (j + 1) * half] = (vown[j] + vrecv[j]).astype(BF16)

    usends[0].wait_recv()
    usends[1].wait_recv()
    solve(0)
    settle(0)
    for p in range(EARLY):
        put(p, half_front(p, 0), 0)
        part_of(p, 0).start()
    usends[2].wait_recv()
    usends[3].wait_recv()
    solve(1)
    settle(1)
    for p in range(EARLY):
        put(p, half_front(p, 1), 1)
        part_of(p, 1).start()

    @pl.loop(EARLY, blocks)
    def _(p):
        block = tab[0, p]
        front = total[block] - jnp.dot(lo[block], solved[...], preferred_element_type=F32)
        put(p, front[:, :half], 0)
        put(p, front[:, half:], 1)
        to_mate(p).start()

    def to_owner(slot):
        return pltpu.make_async_remote_copy(
            src_ref=sbuf.at[slot], dst_ref=land.at[slot], send_sem=ss.at[slot], recv_sem=sr.at[slot],
            device_id=peer(slot), device_id_type=MESH,
        )

    def fill(slot):
        sbuf[slot] = summed[tab[2, slot]]

    def add(p):
        if p < EARLY:
            part_of(p, 0).wait_recv()
            part_of(p, 1).wait_recv()
        else:
            to_mate(p).wait_recv()
        for t in range(2):
            at = slice(t * quarter, (t + 1) * quarter)
            summed[p, :, at] = (keep[p, :, at] + precv[p, t].astype(F32)).astype(BF16)
        fill(p)

    own = pltpu.make_async_copy(sbuf.at[HERE], land.at[HERE], ss.at[HERE])
    for slot in range(FRONTS):
        if slot < blocks:
            add(slot)
        else:
            fill(slot)
        if slot == HERE:
            own.start()
        else:
            to_owner(slot).start()

    for copy in usends + vsends:
        copy.wait_send()
    for p in range(EARLY):
        part_of(p, 0).wait_send()
        part_of(p, 1).wait_send()

    @pl.loop(EARLY, blocks)
    def _(p):
        to_mate(p).wait_send()

    own.wait()
    own_mark.wait()

    for slot in others:
        to_owner(slot).wait()
        mark(slot).wait()


def sketch_call(per_device, bounds, block_map, sketch, upper, pinv, lower, trailing):
    height, width = sketch.shape
    blocks = lower.shape[0] // BLOCK
    pivot = pinv.shape[0]
    half = width // 2
    tiles = 5
    hbm = pl.BlockSpec(memory_space=pltpu.HBM)
    vmem = pl.BlockSpec(memory_space=pltpu.VMEM)
    return pl.pallas_call(
        functools.partial(sketch_kernel, per_device),
        out_shape=(
            jax.ShapeDtypeStruct((FRONTS, BLOCK, half), BF16),
            jax.ShapeDtypeStruct((FRONTS, 8, 128), jnp.int32),
        ),
        in_specs=[pl.BlockSpec(memory_space=pltpu.SMEM), vmem] + [hbm] * 5,
        out_specs=(vmem, vmem),
        scratch_shapes=[
            pltpu.VMEM((8, 128), jnp.int32),
            pltpu.VMEM((8, 128), jnp.int32),
            pltpu.SMEM((8, 128), jnp.int32),
            pltpu.VMEM((height, width), BF16),
            pltpu.VMEM(upper.shape, BF16),
            pltpu.VMEM(pinv.shape, BF16),
            pltpu.VMEM((blocks, BLOCK, pivot), BF16),
            pltpu.VMEM((tiles, trailing.shape[0] // tiles, height), BF16),
            pltpu.VMEM((blocks, BLOCK, width), F32),
            pltpu.VMEM((2, pivot, half), F32),
            pltpu.VMEM((2, pivot, half), BF16),
            pltpu.VMEM((2, pivot, half), BF16),
            pltpu.VMEM((pivot, half), BF16),
            pltpu.VMEM((2, pivot, half), F32),
            pltpu.VMEM((2, pivot, half), F32),
            pltpu.VMEM((pivot, width), BF16),
            pltpu.VMEM((blocks, BLOCK, half), F32),
            pltpu.VMEM((blocks, 2, BLOCK, half // 2), BF16),
            pltpu.VMEM((blocks, 2, BLOCK, half // 2), BF16),
            pltpu.VMEM((blocks, BLOCK, half), BF16),
            pltpu.VMEM((FRONTS, BLOCK, half), BF16),
            pltpu.SemaphoreType.DMA((8 + tiles,)),
            pltpu.SemaphoreType.DMA((4,)),
            pltpu.SemaphoreType.DMA((4,)),
            pltpu.SemaphoreType.DMA((2,)),
            pltpu.SemaphoreType.DMA((2,)),
            pltpu.SemaphoreType.DMA((blocks, 2)),
            pltpu.SemaphoreType.DMA((blocks, 2)),
            pltpu.SemaphoreType.DMA((FRONTS,)),
            pltpu.SemaphoreType.DMA((FRONTS,)),
            pltpu.SemaphoreType.DMA((FRONTS,)),
            pltpu.SemaphoreType.DMA((FRONTS,)),
            pltpu.SemaphoreType.DMA,
        ],
        compiler_params=pltpu.CompilerParams(
            collective_id=0, has_side_effects=True, vmem_limit_bytes=50 * 2**20
        ),
        cost_estimate=pl.CostEstimate(flops=10_000_000_000, bytes_accessed=100_000_000, transcendentals=0),
        name="sketch",
    )(
        bounds, block_map, sketch, upper, pinv,
        lower.reshape(blocks, BLOCK, pivot),
        trailing.reshape(tiles, trailing.shape[0] // tiles, height),
    )


def parent_kernel(tags, land, basis, parent, coeff):
    parent[...] = jnp.zeros_like(parent)
    per = parent.shape[0]

    @pl.loop(0, FRONTS)
    def _(slot):
        tag = tags[slot]

        @pl.when(tag < per)
        def _():
            parent[tag] += land[slot].astype(F32)

    rounded = parent[...].astype(BF16).reshape(per * BLOCK, parent.shape[2])
    coeff[...] = lax.dot_general(
        basis[...], rounded, (((0,), (0,)), ((), ())), preferred_element_type=F32
    )


def parent_call(tags, land, basis):
    rows, rank = basis.shape
    half = land.shape[2]
    vmem = pl.BlockSpec(memory_space=pltpu.VMEM)
    return pl.pallas_call(
        parent_kernel,
        out_shape=(
            jax.ShapeDtypeStruct((rows // BLOCK, BLOCK, half), F32),
            jax.ShapeDtypeStruct((rank, half), F32),
        ),
        in_specs=[pl.BlockSpec(memory_space=pltpu.SMEM), vmem, vmem],
        out_specs=(vmem, vmem),
        compiler_params=pltpu.CompilerParams(vmem_limit_bytes=40 * 2**20),
        name="parent",
    )(tags, land, basis)


def residual_kernel(parent, basis, part, other, out, coeff, tile, total, sems):
    total[...] = part[...] + other[...]
    whole = pltpu.make_async_copy(total, coeff, sems.at[tile.shape[0]])
    whole.start()
    rounded = total[...].astype(BF16)
    rows = tile.shape[1]
    copies = []
    for i in range(tile.shape[0]):
        at = pl.ds(i * rows, rows)
        tile[i] = parent[at, :] - jnp.dot(basis[at, :], rounded, preferred_element_type=F32)
        copy = pltpu.make_async_copy(tile.at[i], out.at[at, :], sems.at[i])
        copy.start()
        copies.append(copy)
    whole.wait()
    for copy in copies:
        copy.wait()


def residual_call(parent, basis, part, other):
    rows, rank = basis.shape
    half = parent.shape[1]
    tile = 256
    vmem = pl.BlockSpec(memory_space=pltpu.VMEM)
    hbm = pl.BlockSpec(memory_space=pltpu.HBM)
    return pl.pallas_call(
        residual_kernel,
        out_shape=(
            jax.ShapeDtypeStruct((rows, half), F32),
            jax.ShapeDtypeStruct((rank, half), F32),
        ),
        in_specs=[vmem] * 4,
        out_specs=(hbm, hbm),
        scratch_shapes=[
            pltpu.VMEM((rows // tile, tile, half), F32),
            pltpu.VMEM((rank, half), F32),
            pltpu.SemaphoreType.DMA((rows // tile + 1,)),
        ],
        compiler_params=pltpu.CompilerParams(vmem_limit_bytes=24 * 2**20),
        name="residual",
    )(parent, basis, part, other)


def body(bounds, block_map, pivot_inverse, upper_block, lower_block, trailing_block, sketch, basis):
    per = basis.shape[1] // BLOCK
    slots = jnp.arange(FRONTS, dtype=jnp.int32)
    land, marks = sketch_call(
        per, bounds, block_map, sketch, upper_block[0], pivot_inverse[0], lower_block[0], trailing_block[0]
    )
    tags = jnp.sum(
        jnp.where(jnp.arange(128, dtype=jnp.int32)[None, :] == slots[:, None], marks[:, 0, :], 0), axis=1
    )
    parent, part = parent_call(tags, land, basis[0])
    other = lax.ppermute(part, "row", [(0, 1), (1, 0)])
    residual, coefficients = residual_call(
        parent.reshape(per * BLOCK, -1), basis[0], part, other
    )
    return coefficients[None], residual[None]


def solution(mesh):
    placed = (
        P("front"),
        P("front", "row"),
        P("front", "col", "row"),
        P("front", "row", "col"),
        P("front", "row", "col"),
        P("front", "row", "col"),
        P("col", None),
        P("front", "row", None),
    )
    return jax.shard_map(
        body,
        mesh=mesh,
        in_specs=placed,
        out_specs=(P("front", None, "col"), P("front", "row", "col")),
        check_vma=False,
    )
```

```python
import functools

import jax
import jax.numpy as jnp
from jax import lax
from jax.experimental import pallas as pl
from jax.experimental.pallas import tpu as pltpu
from jax.sharding import PartitionSpec as P

BLOCK = 128
MESH = pl.DeviceIdType.MESH
F32 = jnp.float32
BF16 = jnp.bfloat16
FRONTS = 32
ORDER = (
    (2, 2, 1), (2, 2, 0), (2, 1, 1), (1, 2, 1), (2, 3, 0), (2, 3, 1), (3, 2, 1), (1, 2, 0), (1, 1, 1), (3, 3, 1),
    (2, 1, 0), (1, 3, 1), (3, 1, 1), (3, 2, 0), (0, 2, 1), (2, 0, 1), (0, 2, 0), (0, 3, 1), (1, 0, 1), (2, 0, 0),
    (3, 0, 1), (1, 1, 0), (3, 3, 0), (0, 1, 1), (1, 3, 0), (3, 1, 0), (0, 0, 1), (0, 1, 0), (1, 0, 0), (0, 3, 0),
    (3, 0, 0), (0, 0, 0),
)
HERE = FRONTS - 1


def total_over(values, axis):
    return jnp.sum(values, axis=axis, keepdims=True)


def tables_of(entries, bound, me, row, per):
    blocks = entries.shape[1]
    down = lax.broadcasted_iota(jnp.int32, (blocks, blocks), 0)
    along = lax.broadcasted_iota(jnp.int32, (blocks, blocks), 1)
    order = lax.broadcasted_iota(jnp.int32, (blocks, 1), 0)
    slots = lax.broadcasted_iota(jnp.int32, (blocks, FRONTS), 1)
    held = total_over(jnp.where(down == along, jnp.broadcast_to(entries, (blocks, blocks)), 0), 1)
    dest = total_over((held >= 2 * per * (slots + 1)).astype(jnp.int32), 1)
    depth, width, near = dest >> 3, (dest >> 1) & 3, dest & 1
    turned = (near + me % 2) & 1
    offset = (((depth - me // 8) & 3) << 3) + (((width - (me // 2) % 4) & 3) << 1) + turned
    slot = jnp.zeros_like(offset)
    for s, (dz, dy, dx) in enumerate(ORDER):
        slot = jnp.where(offset == dz * 8 + dy * 2 + dx, s, slot)
    slot = jnp.where((row * blocks + order) * BLOCK < bound, slot, FRONTS + order)
    wide = jnp.broadcast_to(slot, (blocks, blocks))
    slot_along = total_over(jnp.where(down == along, wide, 0), 0)
    place = total_over((slot_along < wide).astype(jnp.int32), 1)
    at = place == along
    hit = slot == slots
    rest = held - 2 * per * dest
    local = jnp.where(rest >= per, rest - per, rest)
    return (
        total_over(jnp.where(at, down, 0), 0),
        total_over(jnp.where(at, turned, 0), 0),
        total_over(jnp.where(hit, place, 0), 0),
        total_over(jnp.where(hit, local - per, 0), 0) + per,
    )


def sketch_kernel(
    per_device,
    bounds, block_map,
    sk_hbm, up_hbm, pi_hbm, lo_hbm, tr_hbm,
    land, marks,
    tile, tabv, tab, sk, up, pi, lo, tr, total, uown, usend, urecv, piv, vown, vrecv, solved, keep, pay, precv, summed, sbuf,
    ld, us, ur, vs, vr, ps, pr, ss, sr, ms, mr, ts,
):
    me, row, col = lax.axis_index("front"), lax.axis_index("row"), lax.axis_index("col")
    blocks = total.shape[0]
    mate = {"col": 1 - col}
    twin = {"row": 1 - row}

    depth, width = me // 8, (me // 2) % 4
    depths = [((depth + d) % 4) * 8 for d in range(4)]
    widths = [((width + d) % 4) * 2 for d in range(4)]
    near = [me % 2, 1 - me % 2]
    cols = [col, 1 - col]
    others = [slot for slot in range(FRONTS) if slot != HERE]

    def peer(slot):
        dz, dy, dx = ORDER[slot]
        return {"front": depths[dz] + widths[dy] + near[dx], "col": cols[dx]}

    loads = [
        pltpu.make_async_copy(up_hbm, up, ld.at[0]),
        pltpu.make_async_copy(pi_hbm, pi, ld.at[1]),
    ]
    quarter = sk.shape[1] // 4
    tiles = tr.shape[0]
    columns = [
        pltpu.make_async_copy(
            sk_hbm.at[:, pl.ds(q * quarter, quarter)], sk.at[:, pl.ds(i * quarter, quarter)], ld.at[3 + tiles + i]
        )
        for i, q in enumerate((0, 2, 1, 3))
    ]
    for copy in columns:
        copy.start()
    for t in range(tiles):
        loads.append(pltpu.make_async_copy(tr_hbm.at[t], tr.at[t], ld.at[2 + t]))
    loads.append(pltpu.make_async_copy(lo_hbm, lo, ld.at[2 + tiles]))
    for copy in loads:
        copy.start()

    barrier = pltpu.get_barrier_semaphore()
    pl.semaphore_signal(barrier, inc=1, device_id=mate, device_id_type=MESH)
    pl.semaphore_signal(barrier, inc=1, device_id=twin, device_id_type=MESH)

    for slot in others:
        pl.semaphore_signal(barrier, inc=1, device_id=peer(slot), device_id_type=MESH)

    for copy in columns:
        copy.wait()
    height = sk.shape[0]
    bound = bounds[0]
    step = 512

    @pl.loop(0, height // step)
    def _(i):
        at = pl.ds(pl.multiple_of(i * step, step), step)
        places = lax.broadcasted_iota(jnp.int32, (step, sk.shape[1]), 0) + (col * height + i * step)
        sk[at, :] = jnp.where(places < bound, sk[at, :].astype(F32), 0.0).astype(BF16)

    half = sk.shape[1] // 2
    loads[0].wait()
    usends = []
    depth = up.shape[0] // 2
    for j in range(2):
        for h in range(2):
            at = pl.ds(h * depth, depth)
            uown[j, at, :] = jnp.dot(up[at, :], sk[:, j * half : (j + 1) * half], preferred_element_type=F32)
            usend[j, at, :] = uown[j, at, :].astype(BF16)
            if not usends:
                pl.semaphore_wait(barrier, FRONTS + 1)
            copy = pltpu.make_async_remote_copy(
                src_ref=usend.at[j, at], dst_ref=urecv.at[j, at], send_sem=us.at[2 * j + h], recv_sem=ur.at[2 * j + h],
                device_id=mate, device_id_type=MESH,
            )
            copy.start()
            usends.append(copy)

    def mark(slot):
        return pltpu.make_async_remote_copy(
            src_ref=tile, dst_ref=marks.at[slot], send_sem=ms.at[slot], recv_sem=mr.at[slot],
            device_id=peer(slot), device_id_type=MESH,
        )

    rows_of = tables_of(block_map[...], bound, me, row, per_device)
    tile[...] = jnp.zeros_like(tile)
    tile[:, :FRONTS] = jnp.broadcast_to(rows_of[3], (tile.shape[0], FRONTS))
    tabv[...] = jnp.zeros_like(tabv)
    for i in range(3):
        tabv[i : i + 1, : rows_of[i].shape[1]] = rows_of[i]
    to_scalars = pltpu.make_async_copy(tabv, tab, ts)
    to_scalars.start()
    own_mark = pltpu.make_async_copy(tile, marks.at[HERE], ms.at[HERE])
    own_mark.start()
    for slot in others:
        mark(slot).start()

    per = blocks // tiles
    for t in range(tiles):
        loads[2 + t].wait()
        part = jnp.dot(tr[t], sk[...], preferred_element_type=F32)
        total[t * per : (t + 1) * per] = part.reshape(per, BLOCK, 2 * half)

    to_scalars.wait()
    loads[1].wait()
    loads[2 + tiles].wait()

    def part_of(p, t):
        return pltpu.make_async_remote_copy(
            src_ref=pay.at[p, t], dst_ref=precv.at[p, t], send_sem=ps.at[p, t], recv_sem=pr.at[p, t],
            device_id=mate, device_id_type=MESH,
        )

    def put(p, front, t):
        left, right = front[:, :quarter], front[:, quarter:]
        stays = jnp.broadcast_to((tab[1, p] + col) % 2, left.shape) == 0
        keep[p, t] = jnp.where(stays, left, right)
        pay[p, t] = jnp.where(stays, right, left).astype(BF16)

    def half_front(p, t):
        block = tab[0, p]
        at = slice(t * half, (t + 1) * half)
        return total[block, :, at] - jnp.dot(lo[block], solved[:, at], preferred_element_type=F32)

    vsends = []

    def solve(j):
        piv[...] = (uown[j] + urecv[j].astype(F32)).astype(BF16)
        vown[j] = jnp.dot(pi[...], piv[...], preferred_element_type=F32)
        copy = pltpu.make_async_remote_copy(
            src_ref=vown.at[j], dst_ref=vrecv.at[j], send_sem=vs.at[j], recv_sem=vr.at[j],
            device_id=twin, device_id_type=MESH,
        )
        copy.start()
        vsends.append(copy)

    def settle(j):
        vsends[j].wait_recv()
        solved[:, j * half : (j + 1) * half] = (vown[j] + vrecv[j]).astype(BF16)

    for j in range(2):
        usends[2 * j].wait_recv()
        usends[2 * j + 1].wait_recv()
        solve(j)
        settle(j)

        @pl.loop(0, blocks)
        def _(p):
            put(p, half_front(p, j), j)
            part_of(p, j).start()

    def to_owner(slot, t):
        return pltpu.make_async_remote_copy(
            src_ref=sbuf.at[slot, t], dst_ref=land.at[slot, t], send_sem=ss.at[slot, t], recv_sem=sr.at[slot, t],
            device_id=peer(slot), device_id_type=MESH,
        )

    owns = [pltpu.make_async_copy(sbuf.at[HERE, t], land.at[HERE, t], ss.at[HERE, t]) for t in range(2)]
    for t in range(2):
        for slot in range(FRONTS):
            if slot < blocks:
                part_of(slot, t).wait_recv()
                summed[t, slot] = (keep[slot, t] + precv[slot, t].astype(F32)).astype(BF16)
            sbuf[slot, t] = summed[t, tab[2, slot]]
            if slot == HERE:
                owns[t].start()
            else:
                to_owner(slot, t).start()

    for copy in usends + vsends:
        copy.wait_send()

    @pl.loop(0, blocks)
    def _(p):
        part_of(p, 0).wait_send()
        part_of(p, 1).wait_send()

    own_mark.wait()
    for t in range(2):
        owns[t].wait()
        for slot in others:
            to_owner(slot, t).wait()
    for slot in others:
        mark(slot).wait()


def sketch_call(per_device, bounds, block_map, sketch, upper, pinv, lower, trailing):
    height, width = sketch.shape
    blocks = lower.shape[0] // BLOCK
    pivot = pinv.shape[0]
    half = width // 2
    tiles = 5
    hbm = pl.BlockSpec(memory_space=pltpu.HBM)
    vmem = pl.BlockSpec(memory_space=pltpu.VMEM)
    return pl.pallas_call(
        functools.partial(sketch_kernel, per_device),
        out_shape=(
            jax.ShapeDtypeStruct((FRONTS, 2, BLOCK, half // 2), BF16),
            jax.ShapeDtypeStruct((FRONTS, 8, 128), jnp.int32),
        ),
        in_specs=[pl.BlockSpec(memory_space=pltpu.SMEM), vmem] + [hbm] * 5,
        out_specs=(vmem, vmem),
        scratch_shapes=[
            pltpu.VMEM((8, 128), jnp.int32),
            pltpu.VMEM((8, 128), jnp.int32),
            pltpu.SMEM((8, 128), jnp.int32),
            pltpu.VMEM((height, width), BF16),
            pltpu.VMEM(upper.shape, BF16),
            pltpu.VMEM(pinv.shape, BF16),
            pltpu.VMEM((blocks, BLOCK, pivot), BF16),
            pltpu.VMEM((tiles, trailing.shape[0] // tiles, height), BF16),
            pltpu.VMEM((blocks, BLOCK, width), F32),
            pltpu.VMEM((2, pivot, half), F32),
            pltpu.VMEM((2, pivot, half), BF16),
            pltpu.VMEM((2, pivot, half), BF16),
            pltpu.VMEM((pivot, half), BF16),
            pltpu.VMEM((2, pivot, half), F32),
            pltpu.VMEM((2, pivot, half), F32),
            pltpu.VMEM((pivot, width), BF16),
            pltpu.VMEM((blocks, 2, BLOCK, half // 2), F32),
            pltpu.VMEM((blocks, 2, BLOCK, half // 2), BF16),
            pltpu.VMEM((blocks, 2, BLOCK, half // 2), BF16),
            pltpu.VMEM((2, blocks, BLOCK, half // 2), BF16),
            pltpu.VMEM((FRONTS, 2, BLOCK, half // 2), BF16),
            pltpu.SemaphoreType.DMA((8 + tiles,)),
            pltpu.SemaphoreType.DMA((4,)),
            pltpu.SemaphoreType.DMA((4,)),
            pltpu.SemaphoreType.DMA((2,)),
            pltpu.SemaphoreType.DMA((2,)),
            pltpu.SemaphoreType.DMA((blocks, 2)),
            pltpu.SemaphoreType.DMA((blocks, 2)),
            pltpu.SemaphoreType.DMA((FRONTS, 2)),
            pltpu.SemaphoreType.DMA((FRONTS, 2)),
            pltpu.SemaphoreType.DMA((FRONTS,)),
            pltpu.SemaphoreType.DMA((FRONTS,)),
            pltpu.SemaphoreType.DMA,
        ],
        compiler_params=pltpu.CompilerParams(
            collective_id=0, has_side_effects=True, vmem_limit_bytes=50 * 2**20
        ),
        cost_estimate=pl.CostEstimate(flops=10_000_000_000, bytes_accessed=100_000_000, transcendentals=0),
        name="sketch",
    )(
        bounds, block_map, sketch, upper, pinv,
        lower.reshape(blocks, BLOCK, pivot),
        trailing.reshape(tiles, trailing.shape[0] // tiles, height),
    )


def parent_kernel(tags, land, basis, parent, coeff):
    parent[...] = jnp.zeros_like(parent)
    per = parent.shape[0]
    wide = land.shape[3]

    @pl.loop(0, FRONTS)
    def _(slot):
        tag = tags[slot]

        @pl.when(tag < per)
        def _():
            for t in range(2):
                parent[tag, :, t * wide : (t + 1) * wide] += land[slot, t].astype(F32)

    rounded = parent[...].astype(BF16).reshape(per * BLOCK, parent.shape[2])
    coeff[...] = lax.dot_general(
        basis[...], rounded, (((0,), (0,)), ((), ())), preferred_element_type=F32
    )


def parent_call(tags, land, basis):
    rows, rank = basis.shape
    half = 2 * land.shape[3]
    vmem = pl.BlockSpec(memory_space=pltpu.VMEM)
    return pl.pallas_call(
        parent_kernel,
        out_shape=(
            jax.ShapeDtypeStruct((rows // BLOCK, BLOCK, half), F32),
            jax.ShapeDtypeStruct((rank, half), F32),
        ),
        in_specs=[pl.BlockSpec(memory_space=pltpu.SMEM), vmem, vmem],
        out_specs=(vmem, vmem),
        compiler_params=pltpu.CompilerParams(vmem_limit_bytes=40 * 2**20),
        name="parent",
    )(tags, land, basis)


def residual_kernel(parent, basis, part, other, out, coeff, tile, total, sems):
    total[...] = part[...] + other[...]
    whole = pltpu.make_async_copy(total, coeff, sems.at[tile.shape[0]])
    whole.start()
    rounded = total[...].astype(BF16)
    rows = tile.shape[1]
    copies = []
    for i in range(tile.shape[0]):
        at = pl.ds(i * rows, rows)
        tile[i] = parent[at, :] - jnp.dot(basis[at, :], rounded, preferred_element_type=F32)
        copy = pltpu.make_async_copy(tile.at[i], out.at[at, :], sems.at[i])
        copy.start()
        copies.append(copy)
    whole.wait()
    for copy in copies:
        copy.wait()


def residual_call(parent, basis, part, other):
    rows, rank = basis.shape
    half = parent.shape[1]
    tile = 256
    vmem = pl.BlockSpec(memory_space=pltpu.VMEM)
    hbm = pl.BlockSpec(memory_space=pltpu.HBM)
    return pl.pallas_call(
        residual_kernel,
        out_shape=(
            jax.ShapeDtypeStruct((rows, half), F32),
            jax.ShapeDtypeStruct((rank, half), F32),
        ),
        in_specs=[vmem] * 4,
        out_specs=(hbm, hbm),
        scratch_shapes=[
            pltpu.VMEM((rows // tile, tile, half), F32),
            pltpu.VMEM((rank, half), F32),
            pltpu.SemaphoreType.DMA((rows // tile + 1,)),
        ],
        compiler_params=pltpu.CompilerParams(vmem_limit_bytes=24 * 2**20),
        name="residual",
    )(parent, basis, part, other)


def body(bounds, block_map, pivot_inverse, upper_block, lower_block, trailing_block, sketch, basis):
    per = basis.shape[1] // BLOCK
    slots = jnp.arange(FRONTS, dtype=jnp.int32)
    land, marks = sketch_call(
        per, bounds, block_map, sketch, upper_block[0], pivot_inverse[0], lower_block[0], trailing_block[0]
    )
    tags = jnp.sum(
        jnp.where(jnp.arange(128, dtype=jnp.int32)[None, :] == slots[:, None], marks[:, 0, :], 0), axis=1
    )
    parent, part = parent_call(tags, land, basis[0])
    other = lax.ppermute(part, "row", [(0, 1), (1, 0)])
    residual, coefficients = residual_call(
        parent.reshape(per * BLOCK, -1), basis[0], part, other
    )
    return coefficients[None], residual[None]


def solution(mesh):
    placed = (
        P("front"),
        P("front", "row"),
        P("front", "col", "row"),
        P("front", "row", "col"),
        P("front", "row", "col"),
        P("front", "row", "col"),
        P("col", None),
        P("front", "row", None),
    )
    return jax.shard_map(
        body,
        mesh=mesh,
        in_specs=placed,
        out_specs=(P("front", None, "col"), P("front", "row", "col")),
        check_vma=False,
    )
```

```python
import functools

import jax
import jax.numpy as jnp
from jax import lax
from jax.experimental import pallas as pl
from jax.experimental.pallas import tpu as pltpu
from jax.sharding import PartitionSpec as P

BLOCK = 128
MESH = pl.DeviceIdType.MESH
F32 = jnp.float32
BF16 = jnp.bfloat16
FRONTS = 32
ORDER = (
    (2, 2, 1), (2, 2, 0), (2, 1, 1), (1, 2, 1), (2, 3, 0), (2, 3, 1), (3, 2, 1), (1, 2, 0), (1, 1, 1), (3, 3, 1),
    (2, 1, 0), (1, 3, 1), (3, 1, 1), (3, 2, 0), (0, 2, 1), (2, 0, 1), (0, 2, 0), (0, 3, 1), (1, 0, 1), (2, 0, 0),
    (3, 0, 1), (1, 1, 0), (3, 3, 0), (0, 1, 1), (1, 3, 0), (3, 1, 0), (0, 0, 1), (0, 1, 0), (1, 0, 0), (0, 3, 0),
    (3, 0, 0), (0, 0, 0),
)
HERE = FRONTS - 1


def total_over(values, axis):
    return jnp.sum(values, axis=axis, keepdims=True)


def tables_of(entries, bound, me, row, per):
    blocks = entries.shape[1]
    down = lax.broadcasted_iota(jnp.int32, (blocks, blocks), 0)
    along = lax.broadcasted_iota(jnp.int32, (blocks, blocks), 1)
    order = lax.broadcasted_iota(jnp.int32, (blocks, 1), 0)
    slots = lax.broadcasted_iota(jnp.int32, (blocks, FRONTS), 1)
    held = total_over(jnp.where(down == along, jnp.broadcast_to(entries, (blocks, blocks)), 0), 1)
    dest = total_over((held >= 2 * per * (slots + 1)).astype(jnp.int32), 1)
    depth, width, near = dest >> 3, (dest >> 1) & 3, dest & 1
    turned = (near + me % 2) & 1
    offset = (((depth - me // 8) & 3) << 3) + (((width - (me // 2) % 4) & 3) << 1) + turned
    slot = jnp.zeros_like(offset)
    for s, (dz, dy, dx) in enumerate(ORDER):
        slot = jnp.where(offset == dz * 8 + dy * 2 + dx, s, slot)
    slot = jnp.where((row * blocks + order) * BLOCK < bound, slot, FRONTS + order)
    wide = jnp.broadcast_to(slot, (blocks, blocks))
    slot_along = total_over(jnp.where(down == along, wide, 0), 0)
    place = total_over((slot_along < wide).astype(jnp.int32), 1)
    at = place == along
    hit = slot == slots
    rest = held - 2 * per * dest
    local = jnp.where(rest >= per, rest - per, rest)
    return (
        total_over(jnp.where(at, down, 0), 0),
        total_over(jnp.where(at, turned, 0), 0),
        total_over(jnp.where(hit, place, 0), 0),
        total_over(jnp.where(hit, local - per, 0), 0) + per,
    )


def sketch_kernel(
    per_device,
    bounds, block_map,
    sk_hbm, up_hbm, pi_hbm, lo_hbm, tr_hbm,
    land, marks,
    tile, tabv, tab, sk, up, pi, lo, tr, total, uown, usend, urecv, piv, vown, vrecv, solved, keep, pay, precv, summed, sbuf,
    ld, us, ur, vs, vr, ps, pr, ss, sr, ms, mr, ts,
):
    me, row, col = lax.axis_index("front"), lax.axis_index("row"), lax.axis_index("col")
    blocks = total.shape[0]
    mate = {"col": 1 - col}
    twin = {"row": 1 - row}

    depth, width = me // 8, (me // 2) % 4
    depths = [((depth + d) % 4) * 8 for d in range(4)]
    widths = [((width + d) % 4) * 2 for d in range(4)]
    near = [me % 2, 1 - me % 2]
    cols = [col, 1 - col]
    others = [slot for slot in range(FRONTS) if slot != HERE]

    def peer(slot):
        dz, dy, dx = ORDER[slot]
        return {"front": depths[dz] + widths[dy] + near[dx], "col": cols[dx]}

    loads = [
        pltpu.make_async_copy(up_hbm, up, ld.at[0]),
        pltpu.make_async_copy(pi_hbm, pi, ld.at[1]),
    ]
    quarter = sk.shape[1] // 4
    tiles = tr.shape[0]
    columns = [
        pltpu.make_async_copy(
            sk_hbm.at[:, pl.ds(q * quarter, quarter)], sk.at[:, pl.ds(i * quarter, quarter)], ld.at[3 + tiles + i]
        )
        for i, q in enumerate((0, 2, 1, 3))
    ]
    for copy in columns:
        copy.start()
    for t in range(tiles):
        loads.append(pltpu.make_async_copy(tr_hbm.at[t], tr.at[t], ld.at[2 + t]))
    loads.append(pltpu.make_async_copy(lo_hbm, lo, ld.at[2 + tiles]))
    for copy in loads:
        copy.start()

    barrier = pltpu.get_barrier_semaphore()
    pl.semaphore_signal(barrier, inc=1, device_id=mate, device_id_type=MESH)
    pl.semaphore_signal(barrier, inc=1, device_id=twin, device_id_type=MESH)

    for slot in others:
        pl.semaphore_signal(barrier, inc=1, device_id=peer(slot), device_id_type=MESH)

    for copy in columns:
        copy.wait()
    height = sk.shape[0]
    bound = bounds[0]
    step = 512

    @pl.loop(0, height // step)
    def _(i):
        at = pl.ds(pl.multiple_of(i * step, step), step)
        places = lax.broadcasted_iota(jnp.int32, (step, sk.shape[1]), 0) + (col * height + i * step)
        sk[at, :] = jnp.where(places < bound, sk[at, :].astype(F32), 0.0).astype(BF16)

    half = sk.shape[1] // 2
    loads[0].wait()
    usends = []
    depth = up.shape[0] // 2
    for j in range(2):
        for h in range(2):
            at = pl.ds(h * depth, depth)
            uown[j, at, :] = jnp.dot(up[at, :], sk[:, j * half : (j + 1) * half], preferred_element_type=F32)
            usend[j, at, :] = uown[j, at, :].astype(BF16)
            if not usends:
                pl.semaphore_wait(barrier, FRONTS + 1)
            copy = pltpu.make_async_remote_copy(
                src_ref=usend.at[j, at], dst_ref=urecv.at[j, at], send_sem=us.at[2 * j + h], recv_sem=ur.at[2 * j + h],
                device_id=mate, device_id_type=MESH,
            )
            copy.start()
            usends.append(copy)

    def mark(slot):
        return pltpu.make_async_remote_copy(
            src_ref=tile, dst_ref=marks.at[slot], send_sem=ms.at[slot], recv_sem=mr.at[slot],
            device_id=peer(slot), device_id_type=MESH,
        )

    rows_of = tables_of(block_map[...], bound, me, row, per_device)
    tile[...] = jnp.zeros_like(tile)
    tile[:, :FRONTS] = jnp.broadcast_to(rows_of[3], (tile.shape[0], FRONTS))
    tabv[...] = jnp.zeros_like(tabv)
    for i in range(3):
        tabv[i : i + 1, : rows_of[i].shape[1]] = rows_of[i]
    to_scalars = pltpu.make_async_copy(tabv, tab, ts)
    to_scalars.start()
    own_mark = pltpu.make_async_copy(tile, marks.at[HERE], ms.at[HERE])
    own_mark.start()
    for slot in others:
        mark(slot).start()

    per = blocks // tiles
    for t in range(tiles):
        loads[2 + t].wait()
        part = jnp.dot(tr[t], sk[...], preferred_element_type=F32)
        total[t * per : (t + 1) * per] = part.reshape(per, BLOCK, 2 * half)

    to_scalars.wait()
    loads[1].wait()
    loads[2 + tiles].wait()

    def part_of(p, t):
        return pltpu.make_async_remote_copy(
            src_ref=pay.at[p, t], dst_ref=precv.at[p, t], send_sem=ps.at[p, t], recv_sem=pr.at[p, t],
            device_id=mate, device_id_type=MESH,
        )

    def put(p, front, t):
        left, right = front[:, :quarter], front[:, quarter:]
        stays = jnp.broadcast_to((tab[1, p] + col) % 2, left.shape) == 0
        keep[p, t] = jnp.where(stays, left, right)
        pay[p, t] = jnp.where(stays, right, left).astype(BF16)

    def half_front(p, t):
        block = tab[0, p]
        at = slice(t * half, (t + 1) * half)
        return total[block, :, at] - jnp.dot(lo[block], solved[:, at], preferred_element_type=F32)

    vsends = []

    def solve(j):
        piv[...] = (uown[j] + urecv[j].astype(F32)).astype(BF16)
        vown[j] = jnp.dot(pi[...], piv[...], preferred_element_type=F32)
        copy = pltpu.make_async_remote_copy(
            src_ref=vown.at[j], dst_ref=vrecv.at[j], send_sem=vs.at[j], recv_sem=vr.at[j],
            device_id=twin, device_id_type=MESH,
        )
        copy.start()
        vsends.append(copy)

    def settle(j):
        vsends[j].wait_recv()
        solved[:, j * half : (j + 1) * half] = (vown[j] + vrecv[j]).astype(BF16)

    for j in range(2):
        usends[2 * j].wait_recv()
        usends[2 * j + 1].wait_recv()
        solve(j)
        settle(j)

        @pl.loop(0, blocks)
        def _(p):
            put(p, half_front(p, j), j)
            part_of(p, j).start()

    def to_owner(slot, t):
        return pltpu.make_async_remote_copy(
            src_ref=sbuf.at[slot, t], dst_ref=land.at[slot, t], send_sem=ss.at[slot, t], recv_sem=sr.at[slot, t],
            device_id=peer(slot), device_id_type=MESH,
        )

    owns = [pltpu.make_async_copy(sbuf.at[HERE, t], land.at[HERE, t], ss.at[HERE, t]) for t in range(2)]
    for t in range(2):
        for slot in range(FRONTS):
            if slot < blocks:
                part_of(slot, t).wait_recv()
                summed[t, slot] = (keep[slot, t] + precv[slot, t].astype(F32)).astype(BF16)
            sbuf[slot, t] = summed[t, tab[2, slot]]
            if slot == HERE:
                owns[t].start()
            else:
                to_owner(slot, t).start()

    for copy in usends + vsends:
        copy.wait_send()

    @pl.loop(0, blocks)
    def _(p):
        part_of(p, 0).wait_send()
        part_of(p, 1).wait_send()

    own_mark.wait()
    for slot in others:
        mark(slot).wait()
    for t in range(2):
        owns[t].wait()
        for slot in others:
            to_owner(slot, t).wait_send()
            if t == 0:
                to_owner(slot, t).wait_recv()
    for slot in others:
        to_owner(slot, 1).wait_recv()


def sketch_call(per_device, bounds, block_map, sketch, upper, pinv, lower, trailing):
    height, width = sketch.shape
    blocks = lower.shape[0] // BLOCK
    pivot = pinv.shape[0]
    half = width // 2
    tiles = 5
    hbm = pl.BlockSpec(memory_space=pltpu.HBM)
    vmem = pl.BlockSpec(memory_space=pltpu.VMEM)
    return pl.pallas_call(
        functools.partial(sketch_kernel, per_device),
        out_shape=(
            jax.ShapeDtypeStruct((FRONTS, 2, BLOCK, half // 2), BF16),
            jax.ShapeDtypeStruct((FRONTS, 8, 128), jnp.int32),
        ),
        in_specs=[pl.BlockSpec(memory_space=pltpu.SMEM), vmem] + [hbm] * 5,
        out_specs=(vmem, vmem),
        scratch_shapes=[
            pltpu.VMEM((8, 128), jnp.int32),
            pltpu.VMEM((8, 128), jnp.int32),
            pltpu.SMEM((8, 128), jnp.int32),
            pltpu.VMEM((height, width), BF16),
            pltpu.VMEM(upper.shape, BF16),
            pltpu.VMEM(pinv.shape, BF16),
            pltpu.VMEM((blocks, BLOCK, pivot), BF16),
            pltpu.VMEM((tiles, trailing.shape[0] // tiles, height), BF16),
            pltpu.VMEM((blocks, BLOCK, width), F32),
            pltpu.VMEM((2, pivot, half), F32),
            pltpu.VMEM((2, pivot, half), BF16),
            pltpu.VMEM((2, pivot, half), BF16),
            pltpu.VMEM((pivot, half), BF16),
            pltpu.VMEM((2, pivot, half), F32),
            pltpu.VMEM((2, pivot, half), F32),
            pltpu.VMEM((pivot, width), BF16),
            pltpu.VMEM((blocks, 2, BLOCK, half // 2), F32),
            pltpu.VMEM((blocks, 2, BLOCK, half // 2), BF16),
            pltpu.VMEM((blocks, 2, BLOCK, half // 2), BF16),
            pltpu.VMEM((2, blocks, BLOCK, half // 2), BF16),
            pltpu.VMEM((FRONTS, 2, BLOCK, half // 2), BF16),
            pltpu.SemaphoreType.DMA((8 + tiles,)),
            pltpu.SemaphoreType.DMA((4,)),
            pltpu.SemaphoreType.DMA((4,)),
            pltpu.SemaphoreType.DMA((2,)),
            pltpu.SemaphoreType.DMA((2,)),
            pltpu.SemaphoreType.DMA((blocks, 2)),
            pltpu.SemaphoreType.DMA((blocks, 2)),
            pltpu.SemaphoreType.DMA((FRONTS, 2)),
            pltpu.SemaphoreType.DMA((FRONTS, 2)),
            pltpu.SemaphoreType.DMA((FRONTS,)),
            pltpu.SemaphoreType.DMA((FRONTS,)),
            pltpu.SemaphoreType.DMA,
        ],
        compiler_params=pltpu.CompilerParams(
            collective_id=0, has_side_effects=True, vmem_limit_bytes=50 * 2**20
        ),
        cost_estimate=pl.CostEstimate(flops=10_000_000_000, bytes_accessed=100_000_000, transcendentals=0),
        name="sketch",
    )(
        bounds, block_map, sketch, upper, pinv,
        lower.reshape(blocks, BLOCK, pivot),
        trailing.reshape(tiles, trailing.shape[0] // tiles, height),
    )


def parent_kernel(tags, land, basis, parent, coeff):
    parent[...] = jnp.zeros_like(parent)
    per = parent.shape[0]
    wide = land.shape[3]

    @pl.loop(0, FRONTS)
    def _(slot):
        tag = tags[slot]

        @pl.when(tag < per)
        def _():
            for t in range(2):
                parent[tag, :, t * wide : (t + 1) * wide] += land[slot, t].astype(F32)

    rounded = parent[...].astype(BF16).reshape(per * BLOCK, parent.shape[2])
    coeff[...] = lax.dot_general(
        basis[...], rounded, (((0,), (0,)), ((), ())), preferred_element_type=F32
    )


def parent_call(tags, land, basis):
    rows, rank = basis.shape
    half = 2 * land.shape[3]
    vmem = pl.BlockSpec(memory_space=pltpu.VMEM)
    return pl.pallas_call(
        parent_kernel,
        out_shape=(
            jax.ShapeDtypeStruct((rows // BLOCK, BLOCK, half), F32),
            jax.ShapeDtypeStruct((rank, half), F32),
        ),
        in_specs=[pl.BlockSpec(memory_space=pltpu.SMEM), vmem, vmem],
        out_specs=(vmem, vmem),
        compiler_params=pltpu.CompilerParams(vmem_limit_bytes=40 * 2**20),
        name="parent",
    )(tags, land, basis)


def residual_kernel(parent, basis, part, other, out, coeff, tile, total, sems):
    total[...] = part[...] + other[...]
    whole = pltpu.make_async_copy(total, coeff, sems.at[tile.shape[0]])
    whole.start()
    rounded = total[...].astype(BF16)
    rows = tile.shape[1]
    copies = []
    for i in range(tile.shape[0]):
        at = pl.ds(i * rows, rows)
        tile[i] = parent[at, :] - jnp.dot(basis[at, :], rounded, preferred_element_type=F32)
        copy = pltpu.make_async_copy(tile.at[i], out.at[at, :], sems.at[i])
        copy.start()
        copies.append(copy)
    whole.wait()
    for copy in copies:
        copy.wait()


def residual_call(parent, basis, part, other):
    rows, rank = basis.shape
    half = parent.shape[1]
    tile = 256
    vmem = pl.BlockSpec(memory_space=pltpu.VMEM)
    hbm = pl.BlockSpec(memory_space=pltpu.HBM)
    return pl.pallas_call(
        residual_kernel,
        out_shape=(
            jax.ShapeDtypeStruct((rows, half), F32),
            jax.ShapeDtypeStruct((rank, half), F32),
        ),
        in_specs=[vmem] * 4,
        out_specs=(hbm, hbm),
        scratch_shapes=[
            pltpu.VMEM((rows // tile, tile, half), F32),
            pltpu.VMEM((rank, half), F32),
            pltpu.SemaphoreType.DMA((rows // tile + 1,)),
        ],
        compiler_params=pltpu.CompilerParams(vmem_limit_bytes=24 * 2**20),
        name="residual",
    )(parent, basis, part, other)


def body(bounds, block_map, pivot_inverse, upper_block, lower_block, trailing_block, sketch, basis):
    per = basis.shape[1] // BLOCK
    slots = jnp.arange(FRONTS, dtype=jnp.int32)
    land, marks = sketch_call(
        per, bounds, block_map, sketch, upper_block[0], pivot_inverse[0], lower_block[0], trailing_block[0]
    )
    tags = jnp.sum(
        jnp.where(jnp.arange(128, dtype=jnp.int32)[None, :] == slots[:, None], marks[:, 0, :], 0), axis=1
    )
    parent, part = parent_call(tags, land, basis[0])
    other = lax.ppermute(part, "row", [(0, 1), (1, 0)])
    residual, coefficients = residual_call(
        parent.reshape(per * BLOCK, -1), basis[0], part, other
    )
    return coefficients[None], residual[None]


def solution(mesh):
    placed = (
        P("front"),
        P("front", "row"),
        P("front", "col", "row"),
        P("front", "row", "col"),
        P("front", "row", "col"),
        P("front", "row", "col"),
        P("col", None),
        P("front", "row", None),
    )
    return jax.shard_map(
        body,
        mesh=mesh,
        in_specs=placed,
        out_specs=(P("front", None, "col"), P("front", "row", "col")),
        check_vma=False,
    )
```
